512 devices in a mesh: dp: 128 (over y, z, core), panel: 4 (over x).
Axes of the slice: x: 4, y: 4, z: 16, core: 2. Of those that a mesh axis runs over, the one named last changes fastest.
Arguments:
- sample: float32 [32768, 4096], P('dp'), may hold values from -80 to 80
- start_basis: float32 [4096, 512], P('dp', 'panel'), may hold values from -6 to 6
- corpus: float32 [12288, 4096], P('dp'), may hold values from -16 to 16
- owner_shard: int32 [12288, 1], P('dp'), may hold values from 0 to 127; in each aligned block of 96 rows (0 to 95, 96 to 191, ...) at most 2 rows name the same one
Outputs:
- routed: float32 [32768, 512], P('dp', 'panel')
The draws below stay inside these ranges and needn't reach their ends.
Inputs may be any that keep to these rules, and one draw needn't show every extreme that they name: Among the 96 rows of one device at most 2 have the same owner_shard, and in some device exactly 2 do.
All inputs are finite; a program needn't handle non-finite values.
Results may differ from the reference program's by a relative error of at most 0.0003.
Values sent between devices are 32-bit elements; how exact they have to be, the bound alone decides.
No kernel may reach another device: no remote copies, remote signals or barrier semaphores. Data moves between devices by JAX's collectives and lax.ppermute only.
A program may use at most 64 MiB of HBM per device.

```python
import math
import jax
import jax.numpy as jnp
import numpy as np
from jax import lax

D = 4096
K = 512
R_DEV = 96
SAMPLE = 32768
CORPUS = 12288
CAP = 2
ROUTED = 32768
N_DP = 128


def shared_columns(key, low_offset, high_offset, top_log):
    key_offset, key_spread = jax.random.split(jax.random.fold_in(key, 5))
    offset = jax.random.uniform(key_offset, (D,), jnp.float32, low_offset, high_offset)
    spread = jnp.exp(jax.random.uniform(key_spread, (D,), jnp.float32, 0.0, top_log))
    return (offset, spread)


def draw_sample(key, part):
    offset, spread = shared_columns(key, -0.5, 0.5, math.log(3.0))
    key = jax.random.fold_in(key, 11)
    key_noise, key_rows = jax.random.split(key)
    row_index = jnp.arange(SAMPLE, dtype=jnp.float32)
    rising = 1.0 + 2.0 * row_index / max(SAMPLE - 1, 1)
    roughness = jnp.exp(jax.random.uniform(key_rows, (SAMPLE, 1), jnp.float32, 0.0, math.log(2.0)))
    noise_draw = jnp.clip(jax.random.normal(key_noise, (SAMPLE, D), jnp.float32), -4.0, 4.0)
    values = rising[:, None] * roughness * (offset[None, :] + spread[None, :] * noise_draw)
    return values.astype(jnp.float32)


def draw_corpus(key, part):
    offset, spread = shared_columns(key, -0.5, 0.5, math.log(3.0))
    key = jax.random.fold_in(key, 13)
    noise_draw = jnp.clip(jax.random.normal(key, (CORPUS, D), jnp.float32), -4.0, 4.0)
    values = 2.0 / math.log(2.0) * offset[None, :] + spread[None, :] * noise_draw
    return values.astype(jnp.float32)


def level_of(stream_key, dims, shards, low, high):
    level = 1.0
    for dim, parts in shards:
        steps = jax.random.uniform(jax.random.fold_in(jax.random.fold_in(stream_key, 6), dim), (parts,), jnp.float32, low / len(shards), high / len(shards))
        level = level * jnp.repeat(jnp.exp(steps), dims[dim] // parts).reshape((-1,) + (1,) * (len(dims) - 1 - dim))
    return level


def deal_out(key, own, number, rows, amount, top, most, lean):
    sequence = jax.random.permutation(key, amount)
    packed, usual = portions_of(amount, rows * top, most, lean, True), portions_of(amount, rows * top, most, lean, False)
    places = jnp.arange(amount)

    def named(tallies, turn):
        used = int((tallies > 0).sum())
        fixed = max(1, used // 4)
        shifted = fixed + (places - fixed + turn * (used - fixed)) % max(1, amount - fixed)
        return jnp.zeros((amount,), jnp.int32).at[sequence[jnp.where(places < fixed, places, shifted)]].set(jnp.asarray(tallies, jnp.int32))

    tallies = jnp.where(number % 4 == 0, named(packed, number // 4), named(usual, number - number // 4 - 1))
    mixed = jax.random.permutation(jax.random.fold_in(own, 3), amount)
    donor, taker = mixed[0:amount // 2 * 2:2], mixed[1:amount // 2 * 2:2]
    margin = jnp.minimum(tallies[donor] - 1, most - tallies[taker]) // 2
    margin = jnp.where((donor == sequence[0]) | (taker == sequence[0]) | (tallies[taker] == 0), 0, jnp.maximum(margin, 0))
    shifted = jax.random.randint(jax.random.fold_in(own, 4), (amount // 2,), 0, 1 << 20) % (margin + 1)
    tallies = tallies.at[donor].add(-shifted).at[taker].add(shifted)
    members = jnp.searchsorted(jnp.cumsum(tallies), jnp.arange(rows * top), side="right").astype(jnp.int32)
    listing = members.reshape(top, rows).T
    listing = listing[jax.random.permutation(jax.random.fold_in(own, 1), rows)]
    turn = jax.random.randint(jax.random.fold_in(own, 2), (rows, 1), 0, top)
    return jnp.take_along_axis(listing, (jnp.arange(top)[None, :] + turn) % top, axis=1)


def portions_of(amount, total, limit, skew, full):
    loads = [(1 << 20) // math.isqrt(grade ** skew) + 1 for grade in range(1, amount + 1)]
    largest = limit if full else min(limit, max(-(-total // amount), total * loads[0] // sum(loads)))
    least = 1 if total - largest >= amount - 1 else 0
    counts, surplus = [largest] + [least] * (amount - 1), total - largest - least * (amount - 1)
    while surplus > 0:
        movable = [i for i in range(1, amount) if counts[i] < largest] or [i for i in range(1, amount) if counts[i] < limit]
        whole, budget = sum([loads[i] for i in movable]), surplus
        for i in movable:
            addition = min(limit - counts[i], max(1, budget * loads[i] // whole), surplus)
            counts[i] = counts[i] + addition
            surplus = surplus - addition
    return np.array(counts)


def normal_values(own_key, extent, scale, limit, pieces=(), held_as=jnp.bfloat16):
    factor_of = level_of(own_key, extent, pieces, -0.22, 0.18) if pieces else 1.0
    result = jax.random.normal(own_key, extent, jnp.float32) * scale * factor_of
    return jnp.minimum(jnp.maximum(result, -limit), limit).astype(held_as)


def setup_inputs(seed: int = 0) -> dict:
    keys = jax.random.split(jax.random.key(seed), 5)
    sample = draw_sample(jax.random.fold_in(keys[4], 71), 0)
    start_basis = normal_values(keys[1], (D, K), 1.0, 6.0, ((0, 128), (1, 4)), jnp.float32)
    corpus = draw_corpus(jax.random.fold_in(keys[4], 71), 0)
    owner_shard_keys = jax.random.split(jax.random.fold_in(keys[3], 1), CORPUS // R_DEV)
    owner_shard_turns = jax.random.permutation(jax.random.fold_in(keys[3], 3), CORPUS // R_DEV)
    owner_shard = jax.vmap(lambda own, number: deal_out(jax.random.fold_in(keys[3], 2), own, number, R_DEV, N_DP, 1, CAP, 1))(owner_shard_keys, owner_shard_turns).reshape((CORPUS, 1))
    return dict(sample=sample, start_basis=start_basis, corpus=corpus, owner_shard=owner_shard)


def reference(sample, start_basis, corpus, owner_shard):
    highest = lax.Precision.HIGHEST
    col_mean = jnp.sum(sample, axis=0) / SAMPLE
    projected = jnp.dot(sample, start_basis, precision=highest)
    lifted = jnp.dot(col_mean, start_basis, precision=highest)
    image = jnp.dot(sample.T, projected, precision=highest) / SAMPLE - col_mean[:, None] * lifted[None, :]
    gram_matrix = jnp.dot(image.T, image, precision=highest)
    lower_factor = jnp.linalg.cholesky(gram_matrix)
    basis_t = lax.linalg.triangular_solve(lower_factor, image.T, left_side=True, lower=True)
    reduced = jnp.dot(corpus - col_mean[None, :], basis_t.T, precision=highest)
    owners = owner_shard[:, 0].astype(jnp.int32)
    source = (jnp.arange(CORPUS) // R_DEV).astype(jnp.int32)
    onehot = (owners.reshape(N_DP, R_DEV)[:, :, None] == jnp.arange(N_DP).astype(jnp.int32)[None, None, :]).astype(jnp.int32)
    running = jnp.cumsum(onehot, axis=1)
    slot_index = (jnp.sum(running * onehot, axis=2).reshape(-1) - 1).astype(jnp.int32)
    target = (owners * (N_DP * CAP) + source * CAP + slot_index).astype(jnp.int32)
    return jnp.zeros((ROUTED, K), jnp.float32).at[target].set(reduced)
```

```python
import jax
import jax.numpy as jnp
from jax import lax
from jax.sharding import Mesh
from jax.sharding import PartitionSpec as P

DP = ("y", "z", "core")
HIGHEST = lax.Precision.HIGHEST
HIGH = lax.Precision.HIGH


def swap(parts, axis):
    return lax.all_to_all(parts, axis, 0, 0, tiled=True)


def spread(block, axis):
    return swap(jnp.broadcast_to(block[None], (lax.axis_size(axis), *block.shape)), axis)


def pack(*pieces):
    count = pieces[0].shape[0]
    rows = sum(piece.shape[1] for piece in pieces)
    fill = -rows % 8
    if fill:
        pieces += (jnp.zeros((count, fill, pieces[0].shape[2]), jnp.float32),)
    return jnp.concatenate(pieces, axis=1)


def share(row, count):
    return jnp.broadcast_to(row[None], (count, *row.shape))


def in_lanes(values, count, lanes):
    rows = values.reshape(count, -1, min(lanes, values.size // count))
    return jnp.pad(rows, ((0, 0), (0, 0), (0, lanes - rows.shape[2])))


def body(sample, start_basis, corpus, owner_shard):
    ny, nz, nc, np_ = (lax.axis_size(name) for name in (*DP, "panel"))
    owners = ny * nz * nc
    slab, width = start_basis.shape
    depth = slab * owners
    directions = width * np_
    total_rows = sample.shape[0] * owners

    basis = spread(spread(spread(start_basis, "z"), "y"), "core")
    basis = basis.transpose(1, 2, 0, 3, 4).reshape(depth, width)

    column_sums = jnp.sum(sample, axis=0)
    projected = jnp.dot(sample, basis, precision=HIGH)
    lifted = jnp.sum(projected, axis=0, keepdims=True)
    cross = lax.dot_general(sample, projected, (((0,), (0,)), ((), ())), precision=HIGH)

    for axis, count in (("core", nc), ("y", ny), ("z", nz)):
        message = pack(
            cross.reshape(count, -1, width),
            in_lanes(column_sums, count, width),
            share(lifted, count),
        )
        rows = cross.shape[0] // count
        sums = jnp.sum(swap(message, axis), axis=0)
        mean_rows = -(-rows // width)
        cross = sums[:rows]
        column_sums = sums[rows : rows + mean_rows].reshape(-1)[:rows]
        lifted = sums[rows + mean_rows : rows + mean_rows + 1]
    mean = column_sums / total_rows
    image = cross / total_rows - mean[:, None] * (lifted / total_rows)

    image_rows = spread(image, "panel").transpose(1, 0, 2).reshape(slab, directions)
    gram = lax.dot_general(image_rows, image, (((0,), (0,)), ((), ())), precision=HIGHEST)

    rest = directions // owners
    part = directions // nz
    got = swap(
        pack(
            share(image, nz),
            in_lanes(share(mean, nz), nz, width),
            gram.reshape(nz, part, width),
        ),
        "z",
    )
    image = got[:, :slab].reshape(-1, width)
    mean = got[:, slab, :slab].reshape(-1)
    gram = jnp.sum(got[:, slab + 1 : slab + 1 + part], axis=0)
    for axis in ("y", "core"):
        rows = image.shape[0]
        mean_rows = rows // width
        got = spread(
            pack(image[None], in_lanes(mean[None], 1, width), gram[None])[0], axis
        )
        image = got[:, :rows].reshape(-1, width)
        mean = got[:, rows : rows + mean_rows].reshape(-1)
        gram = jnp.sum(got[:, rows + mean_rows : rows + mean_rows + part], axis=0)

    y_index, core_index = lax.axis_index("y"), lax.axis_index("core")
    reduced = jnp.dot(corpus - mean[None, :], image, precision=HIGH)
    corpus_rows = corpus.shape[0]
    capacity = max(2, 2 * corpus_rows // owners)
    owner_ids = owner_shard[:, 0]
    choose = (owner_ids[:, None] == jnp.arange(owners, dtype=jnp.int32)[None, :]).astype(jnp.int32)
    running = jnp.cumsum(choose, axis=0)
    slot_index = jnp.sum(running * choose, axis=1) - 1
    target = owner_ids * capacity + slot_index
    slot_range = jnp.arange(owners * capacity, dtype=jnp.int32)
    placing = (target[None, :] == slot_range[:, None]).astype(jnp.float32)
    outgoing = jnp.dot(placing, reduced, precision=HIGHEST).reshape(owners, capacity, width)

    own_gram = lax.dynamic_slice_in_dim(gram, (y_index * nc + core_index) * rest, rest, 0)
    got = swap(jnp.concatenate([outgoing, share(own_gram, owners)], axis=1), DP)
    routed = got[:, :capacity].reshape(owners * capacity, width)
    gram = got[:, capacity:].reshape(ny, nz, nc, rest, width).transpose(1, 0, 2, 3, 4)
    gram = gram.reshape(directions, width)

    got = spread(jnp.concatenate([gram, routed], axis=0), "panel")
    gram = got[:, :directions].transpose(1, 0, 2).reshape(directions, directions)
    routed = got[:, directions:]
    lower_factor = jnp.linalg.cholesky(gram)
    solved = lax.linalg.triangular_solve(
        lower_factor,
        routed.transpose(0, 2, 1).reshape(directions, owners * capacity),
        left_side=True,
        lower=True,
    )
    own = lax.dynamic_slice_in_dim(solved, lax.axis_index("panel") * width, width, 0)
    return own.T


def solution(mesh):
    y, z, core, panel = 4, 16, 2, mesh.shape["panel"]
    fine = Mesh(mesh.devices.reshape(y, z, core, panel), (*DP, "panel"))
    placed = (P(DP, None), P(DP, "panel"), P(DP, None), P(DP, None))
    return jax.shard_map(
        body, mesh=fine, in_specs=placed, out_specs=P(DP, "panel"), check_vma=False
    )
```

```python
import functools

import jax
import jax.numpy as jnp
from jax import lax
from jax.experimental import pallas as pl
from jax.experimental.pallas import tpu as pltpu
from jax.sharding import Mesh
from jax.sharding import PartitionSpec as P

DP = ("y", "z", "core")
HIGHEST = lax.Precision.HIGHEST
HIGH = lax.Precision.HIGH


def swap(parts, axis):
    return lax.all_to_all(parts, axis, 0, 0, tiled=True)


def spread(block, axis):
    return swap(jnp.broadcast_to(block[None], (lax.axis_size(axis), *block.shape)), axis)


def pack(*pieces):
    count = pieces[0].shape[0]
    rows = sum(piece.shape[1] for piece in pieces)
    fill = -rows % 8
    if fill:
        pieces += (jnp.zeros((count, fill, pieces[0].shape[2]), jnp.float32),)
    return jnp.concatenate(pieces, axis=1)


def share(row, count):
    return jnp.broadcast_to(row[None], (count, *row.shape))


def in_lanes(values, count, lanes):
    rows = values.reshape(count, -1, min(lanes, values.size // count))
    return jnp.pad(rows, ((0, 0), (0, 0), (0, lanes - rows.shape[2])))


def dot_t(a, b):
    return lax.dot_general(
        a, b, (((1,), (1,)), ((), ())), precision=HIGHEST, preferred_element_type=jnp.float32
    )


def invert_factor(block_ref, inverse_ref):
    n = block_ref.shape[0]
    groups = n // 8
    sub = lax.broadcasted_iota(jnp.int32, (8, n), 0)
    lane = lax.broadcasted_iota(jnp.int32, (8, n), 1)

    def full(x):
        return jnp.broadcast_to(x, (8, n))

    left = [block_ref[8 * g : 8 * g + 8, :] for g in range(groups)]
    right = [(lane == sub + 8 * g).astype(jnp.float32) for g in range(groups)]
    for b in range(groups):
        at = 8 * b
        columns = [full(left[b][:, at + i : at + i + 1]) for i in range(8)]
        pivot = [[full(columns[i][j : j + 1, :]) for i in range(j + 1)] for j in range(8)]
        rows = [full(left[b][j : j + 1, :]) for j in range(8)]
        inverse = [full(right[b][j : j + 1, :]) for j in range(8)]
        below = [
            [full(left[g][:, at + i : at + i + 1]) for i in range(8)]
            for g in range(b + 1, groups)
        ]
        scale = []
        for i in range(8):
            scale.append(1.0 / pivot[i][i])
            for j in range(i + 1, 8):
                factor = pivot[j][i] * scale[i]
                for k in range(i + 1, j + 1):
                    pivot[j][k] = pivot[j][k] - factor * pivot[k][i]
                rows[j] = rows[j] - factor * rows[i]
                inverse[j] = inverse[j] - factor * inverse[i]
        for g in range(b + 1, groups):
            column = below[g - b - 1]
            for i in range(8):
                factor = column[i] * scale[i]
                for k in range(i + 1, 8):
                    column[k] = column[k] - factor * pivot[k][i]
                left[g] = left[g] - factor * rows[i]
                right[g] = right[g] - factor * inverse[i]
        done, diagonal = inverse[0], pivot[0][0]
        for j in range(1, 8):
            done = jnp.where(sub == j, inverse[j], done)
            diagonal = jnp.where(sub == j, pivot[j][j], diagonal)
        inverse_ref[at : at + 8, :] = done * lax.rsqrt(diagonal)


def solve_kernel(panel_ref, stacked_ref, out_ref, work_ref, inverse_ref):
    blocks, _, w = work_ref.shape
    kept = out_ref.shape[0]
    work_ref[...] = stacked_ref[...]

    def finish(k):
        solved = dot_t(work_ref[k, (k + 1) * w :, :], inverse_ref[...])
        for m in range(k + 1, blocks):
            at = (m - k - 1) * w
            work_ref[m, m * w :, :] -= dot_t(solved[at:], solved[at : at + w])

        @pl.when(panel_ref[0] == k)
        def _():
            out_ref[...] = solved[-kept:]

    def step(k, carry):
        invert_factor(work_ref.at[k, pl.ds(pl.multiple_of(k * w, w), w)], inverse_ref)
        for q in range(blocks):
            pl.when(k == q)(functools.partial(finish, q))
        return carry

    lax.fori_loop(0, blocks, step, 0)


def solve_rows(panel, stacked, kept):
    blocks, height, w = stacked.shape
    vmem = pl.BlockSpec(memory_space=pltpu.VMEM)
    return pl.pallas_call(
        solve_kernel,
        out_shape=jax.ShapeDtypeStruct((kept, w), jnp.float32),
        in_specs=[pl.BlockSpec(memory_space=pltpu.SMEM), vmem],
        out_specs=vmem,
        scratch_shapes=[
            pltpu.VMEM((blocks, height, w), jnp.float32),
            pltpu.VMEM((w, w), jnp.float32),
        ],
        compiler_params=pltpu.CompilerParams(vmem_limit_bytes=32 << 20),
        cost_estimate=pl.CostEstimate(
            flops=4 * blocks * height * blocks * w * w, bytes_accessed=8 * stacked.size, transcendentals=0
        ),
    )(panel, stacked)


def body(sample, start_basis, corpus, owner_shard):
    ny, nz, nc, np_ = (lax.axis_size(name) for name in (*DP, "panel"))
    owners = ny * nz * nc
    slab, width = start_basis.shape
    depth = slab * owners
    directions = width * np_
    total_rows = sample.shape[0] * owners

    basis = spread(spread(spread(start_basis, "z"), "y"), "core")
    basis = basis.transpose(1, 2, 0, 3, 4).reshape(depth, width)

    column_sums = jnp.sum(sample, axis=0)
    projected = jnp.dot(sample, basis, precision=HIGH)
    lifted = jnp.sum(projected, axis=0, keepdims=True)
    cross = lax.dot_general(sample, projected, (((0,), (0,)), ((), ())), precision=HIGH)

    for axis, count in (("core", nc), ("y", ny), ("z", nz)):
        message = pack(
            cross.reshape(count, -1, width),
            in_lanes(column_sums, count, width),
            share(lifted, count),
        )
        rows = cross.shape[0] // count
        sums = jnp.sum(swap(message, axis), axis=0)
        mean_rows = -(-rows // width)
        cross = sums[:rows]
        column_sums = sums[rows : rows + mean_rows].reshape(-1)[:rows]
        lifted = sums[rows + mean_rows : rows + mean_rows + 1]
    mean = column_sums / total_rows
    image = cross / total_rows - mean[:, None] * (lifted / total_rows)

    image_rows = spread(image, "panel").transpose(1, 0, 2).reshape(slab, directions)
    gram = lax.dot_general(image_rows, image, (((0,), (0,)), ((), ())), precision=HIGHEST)

    rest = directions // owners
    part = directions // nz
    got = swap(
        pack(
            share(image, nz),
            in_lanes(share(mean, nz), nz, width),
            gram.reshape(nz, part, width),
        ),
        "z",
    )
    image = got[:, :slab].reshape(-1, width)
    mean = got[:, slab, :slab].reshape(-1)
    gram = jnp.sum(got[:, slab + 1 : slab + 1 + part], axis=0)
    for axis in ("y", "core"):
        rows = image.shape[0]
        mean_rows = rows // width
        got = spread(
            pack(image[None], in_lanes(mean[None], 1, width), gram[None])[0], axis
        )
        image = got[:, :rows].reshape(-1, width)
        mean = got[:, rows : rows + mean_rows].reshape(-1)
        gram = jnp.sum(got[:, rows + mean_rows : rows + mean_rows + part], axis=0)

    y_index, core_index = lax.axis_index("y"), lax.axis_index("core")
    reduced = jnp.dot(corpus - mean[None, :], image, precision=HIGH)
    corpus_rows = corpus.shape[0]
    capacity = max(2, 2 * corpus_rows // owners)
    owner_ids = owner_shard[:, 0]
    choose = (owner_ids[:, None] == jnp.arange(owners, dtype=jnp.int32)[None, :]).astype(jnp.int32)
    running = jnp.cumsum(choose, axis=0)
    slot_index = jnp.sum(running * choose, axis=1) - 1
    target = owner_ids * capacity + slot_index
    slot_range = jnp.arange(owners * capacity, dtype=jnp.int32)
    placing = (target[None, :] == slot_range[:, None]).astype(jnp.float32)
    outgoing = jnp.dot(placing, reduced, precision=HIGHEST).reshape(owners, capacity, width)

    own_gram = lax.dynamic_slice_in_dim(gram, (y_index * nc + core_index) * rest, rest, 0)
    got = swap(jnp.concatenate([outgoing, share(own_gram, owners)], axis=1), DP)
    routed = got[:, :capacity].reshape(owners * capacity, width)
    gram = got[:, capacity:].reshape(ny, nz, nc, rest, width).transpose(1, 0, 2, 3, 4)
    gram = gram.reshape(directions, width)

    stacked = spread(jnp.concatenate([gram, routed], axis=0), "panel")
    panel = lax.axis_index("panel").astype(jnp.int32).reshape(1)
    return solve_rows(panel, stacked, owners * capacity)


def solution(mesh):
    y, z, core, panel = 4, 16, 2, mesh.shape["panel"]
    fine = Mesh(mesh.devices.reshape(y, z, core, panel), (*DP, "panel"))
    placed = (P(DP, None), P(DP, "panel"), P(DP, None), P(DP, None))
    return jax.shard_map(
        body, mesh=fine, in_specs=placed, out_specs=P(DP, "panel"), check_vma=False
    )
```

```python
import functools

import jax
import jax.numpy as jnp
from jax import lax
from jax.experimental import pallas as pl
from jax.experimental.pallas import tpu as pltpu
from jax.sharding import Mesh
from jax.sharding import PartitionSpec as P

DP = ("y", "z", "core")
HIGHEST = lax.Precision.HIGHEST


def swap(parts, axis):
    return lax.all_to_all(parts, axis, 0, 0, tiled=True)


def spread(block, axis):
    return swap(jnp.broadcast_to(block[None], (lax.axis_size(axis), *block.shape)), axis)


def dot_t(a, b):
    return lax.dot_general(
        a, b, (((1,), (1,)), ((), ())), precision=HIGHEST, preferred_element_type=jnp.float32
    )


def invert_factor(block_ref, inverse_ref):
    n = block_ref.shape[0]
    groups = n // 8
    sub = lax.broadcasted_iota(jnp.int32, (8, n), 0)
    lane = lax.broadcasted_iota(jnp.int32, (8, n), 1)

    def full(x):
        return jnp.broadcast_to(x, (8, n))

    left = [block_ref[8 * g : 8 * g + 8, :] for g in range(groups)]
    right = [(lane == sub + 8 * g).astype(jnp.float32) for g in range(groups)]
    for b in range(groups):
        at = 8 * b
        columns = [full(left[b][:, at + i : at + i + 1]) for i in range(8)]
        pivot = [[full(columns[i][j : j + 1, :]) for i in range(j + 1)] for j in range(8)]
        rows = [full(left[b][j : j + 1, :]) for j in range(8)]
        inverse = [full(right[b][j : j + 1, :]) for j in range(8)]
        below = [
            [full(left[g][:, at + i : at + i + 1]) for i in range(8)]
            for g in range(b + 1, groups)
        ]
        scale = []
        for i in range(8):
            scale.append(1.0 / pivot[i][i])
            for j in range(i + 1, 8):
                factor = pivot[j][i] * scale[i]
                for k in range(i + 1, j + 1):
                    pivot[j][k] = pivot[j][k] - factor * pivot[k][i]
                rows[j] = rows[j] - factor * rows[i]
                inverse[j] = inverse[j] - factor * inverse[i]
        for g in range(b + 1, groups):
            column = below[g - b - 1]
            for i in range(8):
                factor = column[i] * scale[i]
                for k in range(i + 1, 8):
                    column[k] = column[k] - factor * pivot[k][i]
                left[g] = left[g] - factor * rows[i]
                right[g] = right[g] - factor * inverse[i]
        done, diagonal = inverse[0], pivot[0][0]
        for j in range(1, 8):
            done = jnp.where(sub == j, inverse[j], done)
            diagonal = jnp.where(sub == j, pivot[j][j], diagonal)
        inverse_ref[at : at + 8, :] = done * lax.rsqrt(diagonal)


def split(x):
    high = x.astype(jnp.bfloat16)
    return high, (x - high.astype(jnp.float32)).astype(jnp.bfloat16)


def dot_split(a, b, dims):
    (ah, al), (bh, bl) = a, b

    def dot(x, y):
        return lax.dot_general(x, y, (dims, ((), ())), preferred_element_type=jnp.float32)

    return dot(ah, bh) + (dot(ah, bl) + dot(al, bh))


def tdot(a, b):
    return lax.dot_general(
        a, b, (((0,), (0,)), ((), ())), precision=HIGHEST, preferred_element_type=jnp.float32
    )


def up8(rows):
    return -(-rows // 8) * 8


def sample_kernel(sample_ref, basis_ref, out_ref):
    rows, depth = sample_ref.shape
    cores, blocks, slab, w = basis_ref.shape
    tile = 2 * cores * slab * max(1, 128 // (cores * slab))
    per = tile // (cores * slab)
    half = depth // cores
    sums_at = half
    lifted_at = half + half // w
    projected = jnp.zeros((rows, w), jnp.float32)
    for t in range(depth // tile):
        part = jnp.concatenate(
            [basis_ref[c, t * per + i] for i in range(per) for c in range(cores)], axis=0
        )
        columns = split(sample_ref[:, t * tile : (t + 1) * tile])
        projected += dot_split(columns, split(part), ((1,), (0,)))
    lifted = jnp.sum(projected, axis=0, keepdims=True)
    pieces = split(projected)
    for t in range(depth // tile):
        columns = sample_ref[:, t * tile : (t + 1) * tile]
        core, at = t * tile // half, t * tile % half
        out_ref[core, at : at + tile, :] = dot_split(split(columns), pieces, ((0,), (0,)))
        sums = jnp.sum(columns, axis=0, keepdims=True)
        for q in range(tile // w):
            row = sums_at + at // w + q
            out_ref[core, row : row + 1, :] = sums[:, q * w : (q + 1) * w]
    for c in range(cores):
        out_ref[c, lifted_at:, :] = jnp.broadcast_to(lifted, (out_ref.shape[1] - lifted_at, w))


def halve_kernel(got_ref, out_ref):
    count, height, w = out_ref.shape
    rows = got_ref.shape[1]
    main = max(m for m in range(0, rows, w) if m + m // w < rows)
    got = sum(got_ref[i] for i in range(1, got_ref.shape[0])) + got_ref[0]
    lifted = got[main + main // w : main + main // w + 1]
    each, sums = main // count, main // w // count
    for i in range(count):
        out_ref[i, :each, :] = got[i * each : (i + 1) * each]
        out_ref[i, each : each + sums, :] = got[main + i * sums : main + (i + 1) * sums]
        out_ref[i, each + sums :, :] = jnp.broadcast_to(lifted, (height - each - sums, w))


def slab_kernel(slab, got_ref, out_ref):
    count, _, w = out_ref.shape
    got = sum(got_ref[i] for i in range(1, got_ref.shape[0])) + got_ref[0]
    main = slab * count
    in_row = w // slab
    lifted = got[main + main // w : main + main // w + 1]
    lane = lax.broadcasted_iota(jnp.int32, (1, w), 1) // slab
    for i in range(count):
        row = main + i // in_row
        sums = jnp.where(lane == i % in_row, got[row : row + 1], 0.0)
        out_ref[i, :slab, :] = got[i * slab : (i + 1) * slab]
        out_ref[i, slab : slab + 1, :] = sums
        out_ref[i, slab + 1 :, :] = jnp.broadcast_to(lifted, (out_ref.shape[1] - slab - 1, w))


def image_kernel(total_rows, got_ref, spread_ref, own_ref):
    copies, slab, w = spread_ref.shape
    got = sum(got_ref[i] for i in range(1, got_ref.shape[0])) + got_ref[0]
    mean = got[slab : slab + 1] / total_rows
    lifted = got[slab + 1 : slab + 2] / total_rows
    here = lax.broadcasted_iota(jnp.int32, (slab, w), 1) % slab == lax.broadcasted_iota(
        jnp.int32, (slab, w), 0
    )
    column = jnp.sum(jnp.where(here, mean, 0.0), axis=1, keepdims=True)
    image = got[:slab] / total_rows - column * lifted
    for i in range(copies):
        spread_ref[i] = image
    own_ref[:slab, :] = image
    own_ref[slab:, :] = jnp.broadcast_to(mean, (own_ref.shape[0] - slab, w))


def gram_kernel(panel_ref, images_ref, out_ref):
    panel = panel_ref[0]
    w = out_ref.shape[1]
    own, after = images_ref[panel], images_ref[(panel + 1) % 4]
    last = panel == 3
    low = panel % 2
    out_ref[:w, :] = tdot(own, own)
    out_ref[w : 2 * w, :] = tdot(jnp.where(last, own, after), jnp.where(last, after, own))
    across = tdot(images_ref[low + 2], images_ref[low])
    out_ref[2 * w :, :] = jnp.where(panel < 2, across[: w // 2], across[w // 2 :])


def join_kernel(got_ref, own_ref, out_ref):
    gram = sum(got_ref[i] for i in range(1, got_ref.shape[0])) + got_ref[0]
    top = own_ref.shape[0]
    for i in range(out_ref.shape[0]):
        out_ref[i, :top, :] = own_ref[...]
        out_ref[i, top:, :] = gram


def gather_z_kernel(slab, got_ref, out_ref):
    count, height, w = got_ref.shape
    top = slab + 8
    in_row = w // slab
    gram = sum(got_ref[i, top:, :] for i in range(1, count)) + got_ref[0, top:, :]
    main = count * slab
    for c in range(out_ref.shape[0]):
        for i in range(count):
            out_ref[c, i * slab : (i + 1) * slab, :] = got_ref[i, :slab, :]
        for r in range(count // in_row):
            mean = sum(got_ref[r * in_row + q, slab : slab + 1, :] for q in range(in_row))
            out_ref[c, main + r : main + r + 1, :] = mean
        at = out_ref.shape[1] - gram.shape[0]
        for r in range(main + count // in_row, at):
            out_ref[c, r : r + 1, :] = mean
        out_ref[c, at:, :] = gram


def gather_y_kernel(main, sums, share, got_ref, out_ref):
    count = got_ref.shape[0]
    height = out_ref.shape[1]
    for c in range(out_ref.shape[0]):
        for i in range(count):
            out_ref[c, i * main : (i + 1) * main, :] = got_ref[i, :main, :]
            at = count * main + i * sums
            out_ref[c, at : at + sums, :] = got_ref[i, main : main + sums, :]
            at = height - (count - i) * share
            out_ref[c, at : at + share, :] = got_ref[i, got_ref.shape[1] - share :, :]


def corpus_kernel(main, share, got_ref, corpus_ref, out_ref):
    cores, height, w = got_ref.shape
    rows = corpus_ref.shape[0]
    tile = min(main, 4 * w)
    reduced = jnp.zeros((rows, w), jnp.float32)
    for c in range(cores):
        for t in range(main // tile):
            row = main + t * tile // w
            mean = jnp.concatenate(
                [got_ref[c, row + q : row + q + 1, :] for q in range(tile // w)], axis=1
            )
            at = c * main + t * tile
            centered = split(corpus_ref[:, at : at + tile] - mean)
            image = split(got_ref[c, t * tile : (t + 1) * tile, :])
            reduced += dot_split(centered, image, ((1,), (0,)))
    for i in range(out_ref.shape[0]):
        for c in range(cores):
            out_ref[i, c * share : (c + 1) * share, :] = got_ref[c, height - share :, :]
        out_ref[i, cores * share :, :] = reduced


def solve_kernel(panel_ref, target_ref, stacked_ref, out_ref, work_ref, inverse_ref, own_ref):
    blocks, _, w = work_ref.shape
    kept = own_ref.shape[0]
    size = blocks * w
    half = w // 2
    for k in range(blocks):
        work_ref[k, k * w : (k + 1) * w, :] = stacked_ref[k, :w, :]
        work_ref[k, size:, :] = stacked_ref[k, 2 * w + half :, :]
        if k < 3:
            work_ref[k, (k + 1) * w : (k + 2) * w, :] = stacked_ref[k, w : 2 * w, :]
    work_ref[0, 3 * w : 4 * w, :] = stacked_ref[3, w : 2 * w, :]
    for k in range(2):
        for part in range(2):
            at = (k + 2) * w + part * half
            piece = stacked_ref[k + 2 * part, 2 * w : 2 * w + half, :]
            work_ref[k, at : at + half, :] = piece

    def finish(k):
        solved = dot_t(work_ref[k, (k + 1) * w :, :], inverse_ref[...])
        for m in range(k + 1, blocks):
            at = (m - k - 1) * w
            work_ref[m, m * w :, :] -= dot_t(solved[at:], solved[at : at + w])

        @pl.when(panel_ref[0] == k)
        def _():
            own_ref[...] = solved[-kept:]

    def step(k, carry):
        invert_factor(work_ref.at[k, pl.ds(pl.multiple_of(k * w, w), w)], inverse_ref)
        for q in range(blocks):
            pl.when(k == q)(functools.partial(finish, q))
        return carry

    lax.fori_loop(0, blocks, step, 0)
    slots = out_ref.shape[0]
    slot = lax.broadcasted_iota(jnp.int32, (slots, kept), 0)
    placing = (slot == target_ref[...]).astype(jnp.float32)
    out_ref[...] = jnp.dot(
        placing, own_ref[...], precision=HIGHEST, preferred_element_type=jnp.float32
    )


def call(kernel, shapes, *operands, scalars=0, scratch=(), flops=0):
    vmem = pl.BlockSpec(memory_space=pltpu.VMEM)
    smem = pl.BlockSpec(memory_space=pltpu.SMEM)
    outs = [jax.ShapeDtypeStruct(shape, jnp.float32) for shape in shapes]
    moved = 4 * sum(x.size for x in (*operands, *outs))
    got = pl.pallas_call(
        kernel,
        out_shape=outs,
        in_specs=[smem] * scalars + [vmem] * (len(operands) - scalars),
        out_specs=[vmem] * len(outs),
        scratch_shapes=[pltpu.VMEM(shape, jnp.float32) for shape in scratch],
        compiler_params=pltpu.CompilerParams(vmem_limit_bytes=40 << 20),
        cost_estimate=pl.CostEstimate(flops=flops, bytes_accessed=moved, transcendentals=0),
    )(*operands)
    return got if len(outs) > 1 else got[0]


def body(sample, start_basis, corpus, owner_shard):
    ny, nz, nc, panels = (lax.axis_size(name) for name in (*DP, "panel"))
    owners = ny * nz * nc
    slab, w = start_basis.shape
    depth = slab * owners
    rows = sample.shape[0]
    total_rows = rows * owners
    panel = lax.axis_index("panel").astype(jnp.int32).reshape(1)

    basis = spread(spread(spread(start_basis, "z"), "y"), "core")
    basis = basis.reshape(nc, ny * nz, slab, w)

    height = up8(depth // nc + depth // nc // w + 1)
    message = call(sample_kernel, [(nc, height, w)], sample, basis, flops=4 * rows * depth * w)
    main = depth // nc // ny
    message = call(halve_kernel, [(ny, up8(main + main // w + 1), w)], swap(message, "core"))
    message = call(
        functools.partial(slab_kernel, slab), [(nz, slab + 8, w)], swap(message, "y")
    )
    images, own = call(
        functools.partial(image_kernel, float(total_rows)),
        [(panels, slab, w), (slab + 8, w)],
        swap(message, "z"),
    )

    share = 5 * w // 2 // (nc * ny)
    gram = call(gram_kernel, [(5 * w // 2, w)], panel, swap(images, "panel"), scalars=1)
    gram = swap(gram.reshape(nc * ny, share, w), ("core", "y"))
    message = call(join_kernel, [(nz, slab + 8 + share, w)], gram, own)
    sums = main // w
    message = call(
        functools.partial(gather_z_kernel, slab),
        [(ny, main + up8(sums) + share, w)],
        swap(message, "z"),
    )
    message = call(
        functools.partial(gather_y_kernel, main, sums, share),
        [(nc, ny * (main + sums + share), w)],
        swap(message, "y"),
    )

    corpus_rows = corpus.shape[0]
    stacked = call(
        functools.partial(corpus_kernel, ny * main, ny * share),
        [(panels, 5 * w // 2 + corpus_rows, w)],
        swap(message, "core"),
        corpus,
        flops=2 * corpus_rows * depth * w,
    )
    stacked = swap(stacked, "panel")

    capacity = max(2, 2 * corpus_rows // owners)
    owner_ids = owner_shard[:, 0]
    choose = (owner_ids[:, None] == jnp.arange(owners, dtype=jnp.int32)[None, :]).astype(jnp.int32)
    running = jnp.cumsum(choose, axis=0)
    slot_index = jnp.sum(running * choose, axis=1) - 1
    target = (owner_ids * capacity + slot_index)[None, :]
    outgoing = call(
        solve_kernel,
        [(owners * capacity, w)],
        panel,
        target,
        stacked,
        scalars=1,
        scratch=[(panels, panels * w + corpus_rows, w), (w, w), (corpus_rows, w)],
        flops=panels * panels * w * w * (panels * w + corpus_rows),
    )
    arrived = swap(outgoing.reshape(owners, capacity, w), DP)
    return arrived.reshape(owners * capacity, w)


def solution(mesh):
    y, z, core, panel = 4, 16, 2, mesh.shape["panel"]
    fine = Mesh(mesh.devices.reshape(y, z, core, panel), (*DP, "panel"))
    placed = (P(DP, None), P(DP, "panel"), P(DP, None), P(DP, None))
    return jax.shard_map(
        body, mesh=fine, in_specs=placed, out_specs=P(DP, "panel"), check_vma=False
    )
```

```python
import functools

import jax
import jax.numpy as jnp
from jax import lax
from jax.experimental import pallas as pl
from jax.experimental.pallas import tpu as pltpu
from jax.sharding import Mesh
from jax.sharding import PartitionSpec as P

DP = ("y", "z", "core")
HIGHEST = lax.Precision.HIGHEST


def swap(parts, axis):
    return lax.all_to_all(parts, axis, 0, 0, tiled=True)


def spread(block, axis):
    return swap(jnp.broadcast_to(block[None], (lax.axis_size(axis), *block.shape)), axis)


def dot_t(a, b):
    return lax.dot_general(
        a, b, (((1,), (1,)), ((), ())), precision=HIGHEST, preferred_element_type=jnp.float32
    )


def invert_factor(block_ref, inverse_ref):
    n = block_ref.shape[0]
    groups = n // 8
    sub = lax.broadcasted_iota(jnp.int32, (8, n), 0)
    lane = lax.broadcasted_iota(jnp.int32, (8, n), 1)

    def full(x):
        return jnp.broadcast_to(x, (8, n))

    left = [block_ref[8 * g : 8 * g + 8, :] for g in range(groups)]
    right = [(lane == sub + 8 * g).astype(jnp.float32) for g in range(groups)]
    for b in range(groups):
        at = 8 * b
        columns = [full(left[b][:, at + i : at + i + 1]) for i in range(8)]
        pivot = [[full(columns[i][j : j + 1, :]) for i in range(j + 1)] for j in range(8)]
        rows = [full(left[b][j : j + 1, :]) for j in range(8)]
        inverse = [full(right[b][j : j + 1, :]) for j in range(8)]
        below = [
            [full(left[g][:, at + i : at + i + 1]) for i in range(8)]
            for g in range(b + 1, groups)
        ]
        scale = []
        for i in range(8):
            scale.append(1.0 / pivot[i][i])
            for j in range(i + 1, 8):
                factor = pivot[j][i] * scale[i]
                for k in range(i + 1, j + 1):
                    pivot[j][k] = pivot[j][k] - factor * pivot[k][i]
                rows[j] = rows[j] - factor * rows[i]
                inverse[j] = inverse[j] - factor * inverse[i]
        for g in range(b + 1, groups):
            column = below[g - b - 1]
            for i in range(8):
                factor = column[i] * scale[i]
                for k in range(i + 1, 8):
                    column[k] = column[k] - factor * pivot[k][i]
                left[g] = left[g] - factor * rows[i]
                right[g] = right[g] - factor * inverse[i]
        done, diagonal = inverse[0], pivot[0][0]
        for j in range(1, 8):
            done = jnp.where(sub == j, inverse[j], done)
            diagonal = jnp.where(sub == j, pivot[j][j], diagonal)
        inverse_ref[at : at + 8, :] = done * lax.rsqrt(diagonal)


def split(x):
    high = x.astype(jnp.bfloat16)
    return high, (x - high.astype(jnp.float32)).astype(jnp.bfloat16)


def dot_split(a, b, dims):
    (ah, al), (bh, bl) = a, b

    def dot(x, y):
        return lax.dot_general(x, y, (dims, ((), ())), preferred_element_type=jnp.float32)

    return dot(ah, bh) + (dot(ah, bl) + dot(al, bh))


def tdot(a, b):
    return lax.dot_general(
        a, b, (((0,), (0,)), ((), ())), precision=HIGHEST, preferred_element_type=jnp.float32
    )


def up8(rows):
    return -(-rows // 8) * 8


def sample_kernel(sample_ref, basis_ref, out_ref):
    rows, depth = sample_ref.shape
    cores, blocks, slab, w = basis_ref.shape
    tile = 2 * cores * slab * max(1, 128 // (cores * slab))
    per = tile // (cores * slab)
    half = depth // cores
    sums_at = half
    lifted_at = half + half // w
    projected = jnp.zeros((rows, w), jnp.float32)
    for t in range(depth // tile):
        part = jnp.concatenate(
            [basis_ref[c, t * per + i] for i in range(per) for c in range(cores)], axis=0
        )
        columns = split(sample_ref[:, t * tile : (t + 1) * tile])
        projected += dot_split(columns, split(part), ((1,), (0,)))
    lifted = jnp.sum(projected, axis=0, keepdims=True)
    pieces = split(projected)
    for t in range(depth // tile):
        columns = sample_ref[:, t * tile : (t + 1) * tile]
        core, at = t * tile // half, t * tile % half
        out_ref[core, at : at + tile, :] = dot_split(split(columns), pieces, ((0,), (0,)))
        sums = jnp.sum(columns, axis=0, keepdims=True)
        for q in range(tile // w):
            row = sums_at + at // w + q
            out_ref[core, row : row + 1, :] = sums[:, q * w : (q + 1) * w]
    for c in range(cores):
        out_ref[c, lifted_at:, :] = jnp.broadcast_to(lifted, (out_ref.shape[1] - lifted_at, w))


def halve_kernel(got_ref, out_ref):
    count, height, w = out_ref.shape
    rows = got_ref.shape[1]
    main = max(m for m in range(0, rows, w) if m + m // w < rows)
    got = sum(got_ref[i] for i in range(1, got_ref.shape[0])) + got_ref[0]
    lifted = got[main + main // w : main + main // w + 1]
    each, sums = main // count, main // w // count
    for i in range(count):
        out_ref[i, :each, :] = got[i * each : (i + 1) * each]
        out_ref[i, each : each + sums, :] = got[main + i * sums : main + (i + 1) * sums]
        out_ref[i, each + sums :, :] = jnp.broadcast_to(lifted, (height - each - sums, w))


def slab_kernel(slab, got_ref, out_ref):
    count, _, w = out_ref.shape
    got = sum(got_ref[i] for i in range(1, got_ref.shape[0])) + got_ref[0]
    main = slab * count
    in_row = w // slab
    lifted = got[main + main // w : main + main // w + 1]
    lane = lax.broadcasted_iota(jnp.int32, (1, w), 1) // slab
    for i in range(count):
        row = main + i // in_row
        sums = jnp.where(lane == i % in_row, got[row : row + 1], 0.0)
        out_ref[i, :slab, :] = got[i * slab : (i + 1) * slab]
        out_ref[i, slab : slab + 1, :] = sums
        out_ref[i, slab + 1 :, :] = jnp.broadcast_to(lifted, (out_ref.shape[1] - slab - 1, w))


def image_kernel(total_rows, got_ref, spread_ref, own_ref):
    copies, slab, w = spread_ref.shape
    got = sum(got_ref[i] for i in range(1, got_ref.shape[0])) + got_ref[0]
    mean = got[slab : slab + 1] / total_rows
    lifted = got[slab + 1 : slab + 2] / total_rows
    here = lax.broadcasted_iota(jnp.int32, (slab, w), 1) % slab == lax.broadcasted_iota(
        jnp.int32, (slab, w), 0
    )
    column = jnp.sum(jnp.where(here, mean, 0.0), axis=1, keepdims=True)
    image = got[:slab] / total_rows - column * lifted
    for i in range(copies):
        spread_ref[i] = image
    own_ref[:slab, :] = image
    own_ref[slab:, :] = jnp.broadcast_to(mean, (own_ref.shape[0] - slab, w))


def gram_kernel(panel_ref, images_ref, own_ref, out_ref):
    panel = panel_ref[0]
    count, height, w = out_ref.shape
    half, slab = w // 2, images_ref.shape[1]
    own, after = images_ref[panel], images_ref[(panel + 1) % 4]
    last = panel == 3
    low = panel % 2
    square = tdot(own, own)
    row = lax.broadcasted_iota(jnp.int32, (half, w), 0)
    lane = lax.broadcasted_iota(jnp.int32, (half, w), 1)
    folded = jnp.where((lane > row) | (lane >= half), square[:half], pltpu.roll(square[half:], half, 1))
    diagonal = jnp.sum(jnp.where(unit(w), square, 0.0), axis=0, keepdims=True)
    below = tdot(jnp.where(last, own, after), jnp.where(last, after, own))
    across = tdot(images_ref[low + 2], images_ref[low])
    across = jnp.where(panel < 2, across[:half], across[half:])
    gram = jnp.concatenate([folded, below, across], axis=0)
    share = gram.shape[0] // count
    for i in range(count):
        out_ref[i, : slab + 1, :] = own_ref[: slab + 1, :]
        out_ref[i, slab + 1 : slab + 8, :] = jnp.broadcast_to(diagonal, (7, w))
        out_ref[i, slab + 8 :, :] = gram[i * share : (i + 1) * share]


def unit(w):
    row = lax.broadcasted_iota(jnp.int32, (w, w), 0)
    return row == lax.broadcasted_iota(jnp.int32, (w, w), 1)


def total(ref, at, rows):
    return sum(ref[i, at : at + rows, :] for i in range(1, ref.shape[0])) + ref[0, at : at + rows, :]


def gather_z_kernel(got_ref, out_ref):
    count, height, w = got_ref.shape
    _, tall, _ = out_ref.shape
    share = 2 * w // count
    slab = height - 8 - share
    in_row = w // slab
    main, sums = count * slab, count // in_row
    diagonal = total(got_ref, slab + 1, 1)
    gram = total(got_ref, slab + 8, share)
    for c in range(out_ref.shape[0]):
        for i in range(count):
            out_ref[c, i * slab : (i + 1) * slab, :] = got_ref[i, :slab, :]
        for r in range(sums):
            mean = sum(got_ref[r * in_row + q, slab : slab + 1, :] for q in range(in_row))
            out_ref[c, main + r : main + r + 1, :] = mean
        fill = tall - share - main - sums
        out_ref[c, main + sums : tall - share, :] = jnp.broadcast_to(diagonal, (fill, w))
        out_ref[c, tall - share :, :] = gram


def gather_y_kernel(main, sums, share, got_ref, out_ref):
    count, height, w = got_ref.shape
    tall = out_ref.shape[1]
    diagonal = total(got_ref, main + sums, 1)
    gram = total(got_ref, height - share, share)
    for c in range(out_ref.shape[0]):
        for i in range(count):
            out_ref[c, i * main : (i + 1) * main, :] = got_ref[i, :main, :]
            at = count * main + i * sums
            out_ref[c, at : at + sums, :] = got_ref[i, main : main + sums, :]
        at = count * (main + sums)
        out_ref[c, at : tall - share, :] = jnp.broadcast_to(diagonal, (tall - share - at, w))
        out_ref[c, tall - share :, :] = gram


def corpus_kernel(
    main, sums, share, capacity, gram_rows, part_ref, target_ref, got_ref, corpus_ref, out_ref, diagonal_ref
):
    cores, height, w = got_ref.shape
    rows = corpus_ref.shape[0]
    tile = min(main, 4 * w)
    reduced = jnp.zeros((rows, w), jnp.float32)
    for c in range(cores):
        for t in range(main // tile):
            row = main + t * tile // w
            mean = jnp.concatenate(
                [got_ref[c, row + q : row + q + 1, :] for q in range(tile // w)], axis=1
            )
            at = c * main + t * tile
            centered = split(corpus_ref[:, at : at + tile] - mean)
            image = split(got_ref[c, t * tile : (t + 1) * tile, :])
            reduced += dot_split(centered, image, ((1,), (0,)))
    diagonal_ref[...] = jnp.broadcast_to(total(got_ref, main + sums, 1), diagonal_ref.shape)
    gram = total(got_ref, height - share, share)
    tall = up8(gram_rows)
    take = lax.broadcasted_iota(jnp.int32, (tall, share), 1) - part_ref[0] * gram_rows
    take = (take == lax.broadcasted_iota(jnp.int32, (tall, share), 0)).astype(jnp.float32)
    piece = jnp.dot(take, gram, precision=HIGHEST, preferred_element_type=jnp.float32)
    source = jnp.concatenate([reduced, piece], axis=0)
    shape = (out_ref.shape[0], rows + tall)
    row = lax.broadcasted_iota(jnp.int32, shape, 0)
    column = lax.broadcasted_iota(jnp.int32, shape, 1)
    place = lax.rem(row, capacity + gram_rows) - capacity + rows
    slots = (row == target_ref[...]).astype(jnp.float32)
    shares = jnp.where(column < rows, 0.0, (place == column).astype(jnp.float32))
    out_ref[...] = jnp.dot(
        slots + shares, source, precision=HIGHEST, preferred_element_type=jnp.float32
    )


def arrange_kernel(capacity, gram_rows, counts, got_ref, diagonal_ref, out_ref):
    wide = capacity + gram_rows
    owners = got_ref.shape[0] // wide
    top = owners * gram_rows
    ny, nz, nc = counts
    for c in range(out_ref.shape[0]):
        for i in range(owners):
            at = i * wide
            y, z, core = i // (nz * nc), i // nc % nz, i % nc
            row = ((z * ny + y) * nc + core) * gram_rows
            out_ref[c, row : row + gram_rows, :] = got_ref[at + capacity : at + wide, :]
            slot = top + i * capacity
            out_ref[c, slot : slot + capacity, :] = got_ref[at : at + capacity, :]
        out_ref[c, top + owners * capacity :, :] = diagonal_ref[...]


def solve_kernel(panel_ref, stacked_ref, out_ref, work_ref, inverse_ref):
    blocks, _, w = work_ref.shape
    kept = out_ref.shape[0]
    size = blocks * w
    half = w // 2
    height = stacked_ref.shape[1]
    row = lax.broadcasted_iota(jnp.int32, (half, w), 0)
    lane = lax.broadcasted_iota(jnp.int32, (half, w), 1)
    for k in range(blocks):
        folded = stacked_ref[k, :half, :]
        upper = jnp.where((lane > row) | (lane >= half), folded, 0.0)
        moved = pltpu.roll(folded, half, 1)
        lower = jnp.where((lane >= half) & (lane - half < row), moved, 0.0)
        square = jnp.concatenate([upper, lower], axis=0)
        square = square + square.T + jnp.where(unit(w), stacked_ref[k, height - 1 :, :], 0.0)
        work_ref[k, k * w : (k + 1) * w, :] = square
        work_ref[k, size:, :] = stacked_ref[k, 2 * w : 2 * w + kept, :]
        if k < 3:
            work_ref[k, (k + 1) * w : (k + 2) * w, :] = stacked_ref[k, half : half + w, :]
    work_ref[0, 3 * w : 4 * w, :] = stacked_ref[3, half : half + w, :]
    for k in range(2):
        for part in range(2):
            at = (k + 2) * w + part * half
            work_ref[k, at : at + half, :] = stacked_ref[k + 2 * part, half + w : 2 * w, :]

    def finish(k):
        solved = dot_t(work_ref[k, (k + 1) * w :, :], inverse_ref[...])
        for m in range(k + 1, blocks):
            at = (m - k - 1) * w
            work_ref[m, m * w :, :] -= dot_t(solved[at:], solved[at : at + w])

        @pl.when(panel_ref[0] == k)
        def _():
            out_ref[...] = solved[-kept:]

    def step(k, carry):
        invert_factor(work_ref.at[k, pl.ds(pl.multiple_of(k * w, w), w)], inverse_ref)
        for q in range(blocks):
            pl.when(k == q)(functools.partial(finish, q))
        return carry

    lax.fori_loop(0, blocks, step, 0)


def call(kernel, shapes, *operands, scalars=0, scratch=(), flops=0):
    vmem = pl.BlockSpec(memory_space=pltpu.VMEM)
    smem = pl.BlockSpec(memory_space=pltpu.SMEM)
    outs = [jax.ShapeDtypeStruct(shape, jnp.float32) for shape in shapes]
    moved = 4 * sum(x.size for x in (*operands, *outs))
    got = pl.pallas_call(
        kernel,
        out_shape=outs,
        in_specs=[smem] * scalars + [vmem] * (len(operands) - scalars),
        out_specs=[vmem] * len(outs),
        scratch_shapes=[pltpu.VMEM(shape, jnp.float32) for shape in scratch],
        compiler_params=pltpu.CompilerParams(vmem_limit_bytes=40 << 20),
        cost_estimate=pl.CostEstimate(flops=flops, bytes_accessed=moved, transcendentals=0),
    )(*operands)
    return got if len(outs) > 1 else got[0]


def body(sample, start_basis, corpus, owner_shard):
    ny, nz, nc, panels = (lax.axis_size(name) for name in (*DP, "panel"))
    owners = ny * nz * nc
    slab, w = start_basis.shape
    depth = slab * owners
    rows = sample.shape[0]
    total_rows = rows * owners
    panel = lax.axis_index("panel").astype(jnp.int32).reshape(1)

    basis = spread(spread(spread(start_basis, "z"), "y"), "core")
    basis = basis.reshape(nc, ny * nz, slab, w)

    height = up8(depth // nc + depth // nc // w + 1)
    message = call(sample_kernel, [(nc, height, w)], sample, basis, flops=4 * rows * depth * w)
    main = depth // nc // ny
    message = call(halve_kernel, [(ny, up8(main + main // w + 1), w)], swap(message, "core"))
    message = call(
        functools.partial(slab_kernel, slab), [(nz, slab + 8, w)], swap(message, "y")
    )
    images, own = call(
        functools.partial(image_kernel, float(total_rows)),
        [(panels, slab, w), (slab + 8, w)],
        swap(message, "z"),
    )

    share = 2 * w // nz
    message = call(
        gram_kernel,
        [(nz, slab + 8 + share, w)],
        panel,
        swap(images, "panel"),
        own,
        scalars=1,
    )
    sums = main // w
    message = call(gather_z_kernel, [(ny, main + up8(sums + 1) + share, w)], swap(message, "z"))
    message = call(
        functools.partial(gather_y_kernel, main, sums, share),
        [(nc, ny * main + up8(ny * sums + 1) + share, w)],
        swap(message, "y"),
    )

    corpus_rows = corpus.shape[0]
    capacity = max(2, 2 * corpus_rows // owners)
    gram_rows = 2 * w // owners
    wide = capacity + gram_rows
    owner_ids = owner_shard[:, 0]
    choose = (owner_ids[:, None] == jnp.arange(owners, dtype=jnp.int32)[None, :]).astype(jnp.int32)
    running = jnp.cumsum(choose, axis=0)
    slot_index = jnp.sum(running * choose, axis=1) - 1
    target = jnp.pad(owner_ids * wide + slot_index, (0, up8(gram_rows)), constant_values=-1)[None, :]
    part = lax.axis_index("y") * nc + lax.axis_index("core")
    part = part.astype(jnp.int32).reshape(1)
    outgoing, diagonal = call(
        functools.partial(corpus_kernel, ny * main, ny * sums, share, capacity, gram_rows),
        [(owners * wide, w), (8, w)],
        part,
        target,
        swap(message, "core"),
        corpus,
        scalars=1,
        flops=2 * corpus_rows * depth * w,
    )
    arrived = swap(outgoing.reshape(owners, wide, w), DP)
    stacked = call(
        functools.partial(arrange_kernel, capacity, gram_rows, (ny, nz, nc)),
        [(panels, owners * wide + 8, w)],
        arrived.reshape(owners * wide, w),
        diagonal,
    )
    return call(
        solve_kernel,
        [(owners * capacity, w)],
        panel,
        swap(stacked, "panel"),
        scalars=1,
        scratch=[(panels, panels * w + owners * capacity, w), (w, w)],
        flops=panels * panels * w * w * (panels * w + owners * capacity),
    )


def solution(mesh):
    y, z, core, panel = 4, 16, 2, mesh.shape["panel"]
    fine = Mesh(mesh.devices.reshape(y, z, core, panel), (*DP, "panel"))
    placed = (P(DP, None), P(DP, "panel"), P(DP, None), P(DP, None))
    return jax.shard_map(
        body, mesh=fine, in_specs=placed, out_specs=P(DP, "panel"), check_vma=False
    )
```

```python
import functools

import jax
import jax.numpy as jnp
from jax import lax
from jax.experimental import pallas as pl
from jax.experimental.pallas import tpu as pltpu
from jax.sharding import Mesh
from jax.sharding import PartitionSpec as P

DP = ("y", "z", "core")
HIGHEST = lax.Precision.HIGHEST


def swap(parts, axis):
    return lax.all_to_all(parts, axis, 0, 0, tiled=True)


def spread(block, axis):
    return swap(jnp.broadcast_to(block[None], (lax.axis_size(axis), *block.shape)), axis)


def dot_t(a, b):
    return lax.dot_general(
        a, b, (((1,), (1,)), ((), ())), precision=HIGHEST, preferred_element_type=jnp.float32
    )


def invert_factor(block_ref, inverse_ref):
    n = block_ref.shape[0]
    groups = n // 8
    sub = lax.broadcasted_iota(jnp.int32, (8, n), 0)
    lane = lax.broadcasted_iota(jnp.int32, (8, n), 1)

    def full(x):
        return jnp.broadcast_to(x, (8, n))

    left = [block_ref[8 * g : 8 * g + 8, :] for g in range(groups)]
    right = [(lane == sub + 8 * g).astype(jnp.float32) for g in range(groups)]
    for b in range(groups):
        at = 8 * b
        columns = [full(left[b][:, at + i : at + i + 1]) for i in range(8)]
        pivot = [[full(columns[i][j : j + 1, :]) for i in range(j + 1)] for j in range(8)]
        rows = [full(left[b][j : j + 1, :]) for j in range(8)]
        inverse = [full(right[b][j : j + 1, :]) for j in range(8)]
        below = [
            [full(left[g][:, at + i : at + i + 1]) for i in range(8)]
            for g in range(b + 1, groups)
        ]
        scale = []
        for i in range(8):
            scale.append(1.0 / pivot[i][i])
            for j in range(i + 1, 8):
                factor = pivot[j][i] * scale[i]
                for k in range(i + 1, j + 1):
                    pivot[j][k] = pivot[j][k] - factor * pivot[k][i]
                rows[j] = rows[j] - factor * rows[i]
                inverse[j] = inverse[j] - factor * inverse[i]
        for g in range(b + 1, groups):
            column = below[g - b - 1]
            for i in range(8):
                factor = column[i] * scale[i]
                for k in range(i + 1, 8):
                    column[k] = column[k] - factor * pivot[k][i]
                left[g] = left[g] - factor * rows[i]
                right[g] = right[g] - factor * inverse[i]
        done, diagonal = inverse[0], pivot[0][0]
        for j in range(1, 8):
            done = jnp.where(sub == j, inverse[j], done)
            diagonal = jnp.where(sub == j, pivot[j][j], diagonal)
        inverse_ref[at : at + 8, :] = done * lax.rsqrt(diagonal)


def split(x):
    high = x.astype(jnp.bfloat16)
    return high, (x - high.astype(jnp.float32)).astype(jnp.bfloat16)


def dot_split(a, b, dims):
    (ah, al), (bh, bl) = a, b

    def dot(x, y):
        return lax.dot_general(x, y, (dims, ((), ())), preferred_element_type=jnp.float32)

    return dot(ah, bh) + (dot(ah, bl) + dot(al, bh))


def tdot(a, b):
    return lax.dot_general(
        a, b, (((0,), (0,)), ((), ())), precision=HIGHEST, preferred_element_type=jnp.float32
    )


def up8(rows):
    return -(-rows // 8) * 8


def sample_kernel(sample_ref, basis_ref, out_ref):
    rows, depth = sample_ref.shape
    cores, blocks, slab, w = basis_ref.shape
    tile = 2 * cores * slab * max(1, 128 // (cores * slab))
    per = tile // (cores * slab)
    half = depth // cores
    sums_at = half
    lifted_at = half + half // w
    projected = jnp.zeros((rows, w), jnp.float32)
    for t in range(depth // tile):
        part = jnp.concatenate(
            [basis_ref[c, t * per + i] for i in range(per) for c in range(cores)], axis=0
        )
        columns = split(sample_ref[:, t * tile : (t + 1) * tile])
        projected += dot_split(columns, split(part), ((1,), (0,)))
    lifted = jnp.sum(projected, axis=0, keepdims=True)
    pieces = split(projected)
    for t in range(depth // tile):
        columns = sample_ref[:, t * tile : (t + 1) * tile]
        core, at = t * tile // half, t * tile % half
        out_ref[core, at : at + tile, :] = dot_split(split(columns), pieces, ((0,), (0,)))
        sums = jnp.sum(columns, axis=0, keepdims=True)
        for q in range(tile // w):
            row = sums_at + at // w + q
            out_ref[core, row : row + 1, :] = sums[:, q * w : (q + 1) * w]
    for c in range(cores):
        out_ref[c, lifted_at:, :] = jnp.broadcast_to(lifted, (out_ref.shape[1] - lifted_at, w))


def halve_kernel(got_ref, out_ref):
    count, height, w = out_ref.shape
    rows = got_ref.shape[1]
    main = max(m for m in range(0, rows, w) if m + m // w < rows)
    got = sum(got_ref[i] for i in range(1, got_ref.shape[0])) + got_ref[0]
    lifted = got[main + main // w : main + main // w + 1]
    each, sums = main // count, main // w // count
    for i in range(count):
        out_ref[i, :each, :] = got[i * each : (i + 1) * each]
        out_ref[i, each : each + sums, :] = got[main + i * sums : main + (i + 1) * sums]
        out_ref[i, each + sums :, :] = jnp.broadcast_to(lifted, (height - each - sums, w))


def slab_kernel(slab, got_ref, out_ref):
    count, _, w = out_ref.shape
    got = sum(got_ref[i] for i in range(1, got_ref.shape[0])) + got_ref[0]
    main = slab * count
    in_row = w // slab
    lifted = got[main + main // w : main + main // w + 1]
    lane = lax.broadcasted_iota(jnp.int32, (1, w), 1) // slab
    for i in range(count):
        row = main + i // in_row
        sums = jnp.where(lane == i % in_row, got[row : row + 1], 0.0)
        out_ref[i, :slab, :] = got[i * slab : (i + 1) * slab]
        out_ref[i, slab : slab + 1, :] = sums
        out_ref[i, slab + 1 :, :] = jnp.broadcast_to(lifted, (out_ref.shape[1] - slab - 1, w))


def image_kernel(total_rows, got_ref, spread_ref, own_ref):
    copies, slab, w = spread_ref.shape
    got = sum(got_ref[i] for i in range(1, got_ref.shape[0])) + got_ref[0]
    mean = got[slab : slab + 1] / total_rows
    lifted = got[slab + 1 : slab + 2] / total_rows
    here = lax.broadcasted_iota(jnp.int32, (slab, w), 1) % slab == lax.broadcasted_iota(
        jnp.int32, (slab, w), 0
    )
    column = jnp.sum(jnp.where(here, mean, 0.0), axis=1, keepdims=True)
    image = got[:slab] / total_rows - column * lifted
    for i in range(copies):
        spread_ref[i] = image
    own_ref[:slab, :] = image
    own_ref[slab:, :] = jnp.broadcast_to(mean, (own_ref.shape[0] - slab, w))


def gram_kernel(pieces, panel_ref, images_ref, own_ref, out_ref, gram_ref):
    panel = panel_ref[0]
    count, height, w = out_ref.shape
    half, slab = w // 2, images_ref.shape[1]
    own, after = images_ref[panel], images_ref[(panel + 1) % 4]
    last = panel == 3
    low = panel % 2
    square = tdot(own, own)
    row = lax.broadcasted_iota(jnp.int32, (half, w), 0)
    lane = lax.broadcasted_iota(jnp.int32, (half, w), 1)
    folded = jnp.where((lane > row) | (lane >= half), square[:half], pltpu.roll(square[half:], half, 1))
    diagonal = jnp.sum(jnp.where(unit(w), square, 0.0), axis=0, keepdims=True)
    below = tdot(jnp.where(last, own, after), jnp.where(last, after, own))
    across = tdot(images_ref[low + 2], images_ref[low])
    across = jnp.where(panel < 2, across[:half], across[half:])
    gram_ref[...] = jnp.concatenate([folded, below, across], axis=0)
    each = gram_ref.shape[0] // count // pieces
    for i in range(count):
        out_ref[i, : slab + 1, :] = own_ref[: slab + 1, :]
        out_ref[i, slab + 1 : slab + 8, :] = jnp.broadcast_to(diagonal, (7, w))
        for q in range(pieces):
            at, row = slab + 8 + q * each, (q * count + i) * each
            out_ref[i, at : at + each, :] = gram_ref[row : row + each, :]


def unit(w):
    row = lax.broadcasted_iota(jnp.int32, (w, w), 0)
    return row == lax.broadcasted_iota(jnp.int32, (w, w), 1)


def total(ref, at, rows):
    return sum(ref[i, at : at + rows, :] for i in range(1, ref.shape[0])) + ref[0, at : at + rows, :]


def gather_z_kernel(got_ref, out_ref):
    count, height, w = got_ref.shape
    _, tall, _ = out_ref.shape
    share = 2 * w // count
    slab = height - 8 - share
    in_row = w // slab
    main, sums = count * slab, count // in_row
    diagonal = total(got_ref, slab + 1, 1)
    gram = total(got_ref, slab + 8, share)
    for c in range(out_ref.shape[0]):
        for i in range(count):
            out_ref[c, i * slab : (i + 1) * slab, :] = got_ref[i, :slab, :]
        for r in range(sums):
            mean = sum(got_ref[r * in_row + q, slab : slab + 1, :] for q in range(in_row))
            out_ref[c, main + r : main + r + 1, :] = mean
        fill = tall - share - main - sums
        out_ref[c, main + sums : tall - share, :] = jnp.broadcast_to(diagonal, (fill, w))
        out_ref[c, tall - share :, :] = gram


def gather_y_kernel(main, sums, share, got_ref, out_ref):
    count, height, w = got_ref.shape
    tall = out_ref.shape[1]
    diagonal = total(got_ref, main + sums, 1)
    gram = total(got_ref, height - share, share)
    for c in range(out_ref.shape[0]):
        for i in range(count):
            out_ref[c, i * main : (i + 1) * main, :] = got_ref[i, :main, :]
            at = count * main + i * sums
            out_ref[c, at : at + sums, :] = got_ref[i, main : main + sums, :]
        at = count * (main + sums)
        out_ref[c, at : tall - share, :] = jnp.broadcast_to(diagonal, (tall - share - at, w))
        out_ref[c, tall - share :, :] = gram


def corpus_kernel(
    main, sums, share, lead, height_out, gram_rows, part_ref, target_ref, got_ref, corpus_ref, out_ref, diagonal_ref
):
    cores, height, w = got_ref.shape
    rows = corpus_ref.shape[0]
    tile = min(main, 4 * w)
    reduced = jnp.zeros((rows, w), jnp.float32)
    for c in range(cores):
        for t in range(main // tile):
            row = main + t * tile // w
            mean = jnp.concatenate(
                [got_ref[c, row + q : row + q + 1, :] for q in range(tile // w)], axis=1
            )
            at = c * main + t * tile
            centered = split(corpus_ref[:, at : at + tile] - mean)
            image = split(got_ref[c, t * tile : (t + 1) * tile, :])
            reduced += dot_split(centered, image, ((1,), (0,)))
    diagonal_ref[...] = jnp.broadcast_to(total(got_ref, main + sums, 1), diagonal_ref.shape)
    gram = total(got_ref, height - share, share)
    tall = up8(gram_rows)
    take = lax.broadcasted_iota(jnp.int32, (tall, share), 1) - part_ref[0] * gram_rows
    take = (take == lax.broadcasted_iota(jnp.int32, (tall, share), 0)).astype(jnp.float32)
    piece = jnp.dot(take, gram, precision=HIGHEST, preferred_element_type=jnp.float32)
    source = jnp.concatenate([reduced, piece], axis=0)
    shape = (out_ref.shape[0], rows + tall)
    row = lax.broadcasted_iota(jnp.int32, shape, 0)
    column = lax.broadcasted_iota(jnp.int32, shape, 1)
    place = lax.rem(row, height_out) - lead + rows
    slots = (row == target_ref[...]).astype(jnp.float32)
    shares = jnp.where(column < rows, 0.0, (place == column).astype(jnp.float32))
    out_ref[...] = jnp.dot(
        slots + shares, source, precision=HIGHEST, preferred_element_type=jnp.float32
    )


def arrange_kernel(capacity, gram_rows, got_ref, diagonal_ref, out_ref):
    count = got_ref.shape[0]
    peers = out_ref.shape[0]
    panels = 4
    lead = peers // panels * capacity
    top = count * capacity
    full = top + count * gram_rows
    for i in range(count):
        for q in range(peers // panels):
            rows = got_ref[i, q * capacity : (q + 1) * capacity, :]
            out_ref[q * panels, i * capacity : (i + 1) * capacity, :] = rows
        rows = got_ref[i, lead : lead + gram_rows, :]
        out_ref[0, top + i * gram_rows : top + (i + 1) * gram_rows, :] = rows
    for q in range(peers):
        first = q // panels * panels
        if q != first:
            out_ref[q, :top, :] = out_ref[first, :top, :]
        if q:
            out_ref[q, top:full, :] = out_ref[0, top:full, :]
        out_ref[q, full:, :] = diagonal_ref[...]


def solve_kernel(
    counts, panel_ref, got_ref, out_ref, work_ref, inverse_ref, stacked_ref, own_ref
):
    blocks, _, w = work_ref.shape
    kept = out_ref.shape[0]
    size = blocks * w
    half = w // 2
    ny, nz, nc = counts
    top = kept // (ny * nc)
    share = 2 * w // (ny * nc)
    row = lax.broadcasted_iota(jnp.int32, (half, w), 0)
    lane = lax.broadcasted_iota(jnp.int32, (half, w), 1)
    for k in range(blocks):
        for q in range(ny * nc):
            source = q * blocks + k
            stacked_ref[k, q * share : (q + 1) * share, :] = got_ref[source, top : top + share, :]
            at = size + q * top
            work_ref[k, at : at + top, :] = got_ref[source, :top, :]
        folded = stacked_ref[k, :half, :]
        upper = jnp.where((lane > row) | (lane >= half), folded, 0.0)
        moved = pltpu.roll(folded, half, 1)
        lower = jnp.where((lane >= half) & (lane - half < row), moved, 0.0)
        square = jnp.concatenate([upper, lower], axis=0)
        diagonal = got_ref[k, top + share : top + share + 1, :]
        square = square + square.T + jnp.where(unit(w), diagonal, 0.0)
        work_ref[k, k * w : (k + 1) * w, :] = square
        if k < 3:
            work_ref[k, (k + 1) * w : (k + 2) * w, :] = stacked_ref[k, half : half + w, :]
    work_ref[0, 3 * w : 4 * w, :] = stacked_ref[3, half : half + w, :]
    for k in range(2):
        for part in range(2):
            at = (k + 2) * w + part * half
            work_ref[k, at : at + half, :] = stacked_ref[k + 2 * part, half + w : 2 * w, :]

    def finish(k):
        solved = dot_t(work_ref[k, (k + 1) * w :, :], inverse_ref[...])
        for m in range(k + 1, blocks):
            at = (m - k - 1) * w
            work_ref[m, m * w :, :] -= dot_t(solved[at:], solved[at : at + w])

        @pl.when(panel_ref[0] == k)
        def _():
            own_ref[...] = solved[-kept:]

    def step(k, carry):
        invert_factor(work_ref.at[k, pl.ds(pl.multiple_of(k * w, w), w)], inverse_ref)
        for q in range(blocks):
            pl.when(k == q)(functools.partial(finish, q))
        return carry

    lax.fori_loop(0, blocks, step, 0)
    slots = kept // (ny * nz * nc)
    for i in range(ny * nz * nc):
        y, z, core = i // (nz * nc), i // nc % nz, i % nc
        at = ((y * nc + core) * nz + z) * slots
        out_ref[i * slots : (i + 1) * slots, :] = own_ref[at : at + slots, :]


def call(kernel, shapes, *operands, scalars=0, scratch=(), flops=0):
    vmem = pl.BlockSpec(memory_space=pltpu.VMEM)
    smem = pl.BlockSpec(memory_space=pltpu.SMEM)
    outs = [jax.ShapeDtypeStruct(shape, jnp.float32) for shape in shapes]
    moved = 4 * sum(x.size for x in (*operands, *outs))
    got = pl.pallas_call(
        kernel,
        out_shape=outs,
        in_specs=[smem] * scalars + [vmem] * (len(operands) - scalars),
        out_specs=[vmem] * len(outs),
        scratch_shapes=[pltpu.VMEM(shape, jnp.float32) for shape in scratch],
        compiler_params=pltpu.CompilerParams(vmem_limit_bytes=40 << 20),
        cost_estimate=pl.CostEstimate(flops=flops, bytes_accessed=moved, transcendentals=0),
    )(*operands)
    return got if len(outs) > 1 else got[0]


def body(sample, start_basis, corpus, owner_shard):
    ny, nz, nc, panels = (lax.axis_size(name) for name in (*DP, "panel"))
    owners = ny * nz * nc
    slab, w = start_basis.shape
    depth = slab * owners
    rows = sample.shape[0]
    total_rows = rows * owners
    panel = lax.axis_index("panel").astype(jnp.int32).reshape(1)

    basis = spread(spread(spread(start_basis, "z"), "y"), "core")
    basis = basis.reshape(nc, ny * nz, slab, w)

    height = up8(depth // nc + depth // nc // w + 1)
    message = call(sample_kernel, [(nc, height, w)], sample, basis, flops=4 * rows * depth * w)
    main = depth // nc // ny
    message = call(halve_kernel, [(ny, up8(main + main // w + 1), w)], swap(message, "core"))
    message = call(
        functools.partial(slab_kernel, slab), [(nz, slab + 8, w)], swap(message, "y")
    )
    images, own = call(
        functools.partial(image_kernel, float(total_rows)),
        [(panels, slab, w), (slab + 8, w)],
        swap(message, "z"),
    )

    share = 2 * w // nz
    message = call(
        functools.partial(gram_kernel, ny * nc),
        [(nz, slab + 8 + share, w)],
        panel,
        swap(images, "panel"),
        own,
        scalars=1,
        scratch=[(2 * w, w)],
    )
    sums = main // w
    message = call(gather_z_kernel, [(ny, main + up8(sums + 1) + share, w)], swap(message, "z"))
    message = call(
        functools.partial(gather_y_kernel, main, sums, share),
        [(nc, ny * main + up8(ny * sums + 1) + share, w)],
        swap(message, "y"),
    )

    corpus_rows = corpus.shape[0]
    capacity = max(2, 2 * corpus_rows // owners)
    gram_rows = 2 * w // owners
    lead = ny * nc * capacity
    height = up8(lead + gram_rows)
    owner_ids = owner_shard[:, 0]
    choose = (owner_ids[:, None] == jnp.arange(owners, dtype=jnp.int32)[None, :]).astype(jnp.int32)
    running = jnp.cumsum(choose, axis=0)
    slot_index = jnp.sum(running * choose, axis=1) - 1
    plane = owner_ids // (nz * nc) * nc + owner_ids % nc
    target = owner_ids // nc % nz * height + plane * capacity + slot_index
    target = jnp.pad(target, (0, up8(gram_rows)), constant_values=-1)[None, :]
    part = lax.axis_index("y") * nc + lax.axis_index("core")
    part = part.astype(jnp.int32).reshape(1)
    outgoing, diagonal = call(
        functools.partial(corpus_kernel, ny * main, ny * sums, share, lead, height, gram_rows),
        [(nz * height, w), (8, w)],
        part,
        target,
        swap(message, "core"),
        corpus,
        scalars=1,
        flops=2 * corpus_rows * depth * w,
    )
    message = call(
        functools.partial(arrange_kernel, capacity, gram_rows),
        [(ny * nc * panels, nz * (capacity + gram_rows) + 8, w)],
        swap(outgoing.reshape(nz, height, w), "z"),
        diagonal,
    )
    slots = owners * capacity
    return call(
        functools.partial(solve_kernel, (ny, nz, nc)),
        [(slots, w)],
        panel,
        swap(message, ("y", "core", "panel")),
        scalars=1,
        scratch=[(panels, panels * w + slots, w), (w, w), (panels, 2 * w, w), (slots, w)],
        flops=panels * panels * w * w * (panels * w + slots),
    )


def solution(mesh):
    y, z, core, panel = 4, 16, 2, mesh.shape["panel"]
    fine = Mesh(mesh.devices.reshape(y, z, core, panel), (*DP, "panel"))
    placed = (P(DP, None), P(DP, "panel"), P(DP, None), P(DP, None))
    return jax.shard_map(
        body, mesh=fine, in_specs=placed, out_specs=P(DP, "panel"), check_vma=False
    )
```

```python
import functools

import jax
import jax.numpy as jnp
from jax import lax
from jax.experimental import pallas as pl
from jax.experimental.pallas import tpu as pltpu
from jax.sharding import Mesh
from jax.sharding import PartitionSpec as P

DP = ("y", "z", "core")
HIGHEST = lax.Precision.HIGHEST


def swap(parts, axis):
    return lax.all_to_all(parts, axis, 0, 0, tiled=True)


def spread(block, axis):
    return swap(jnp.broadcast_to(block[None], (lax.axis_size(axis), *block.shape)), axis)


def dot_t(a, b):
    return lax.dot_general(
        a, b, (((1,), (1,)), ((), ())), precision=HIGHEST, preferred_element_type=jnp.float32
    )


def invert_factor(block_ref, inverse_ref):
    n = block_ref.shape[0]
    groups = n // 8
    sub = lax.broadcasted_iota(jnp.int32, (8, n), 0)
    lane = lax.broadcasted_iota(jnp.int32, (8, n), 1)

    def full(x):
        return jnp.broadcast_to(x, (8, n))

    left = [block_ref[8 * g : 8 * g + 8, :] for g in range(groups)]
    right = [(lane == sub + 8 * g).astype(jnp.float32) for g in range(groups)]
    for b in range(groups):
        at = 8 * b
        columns = [full(left[b][:, at + i : at + i + 1]) for i in range(8)]
        pivot = [[full(columns[i][j : j + 1, :]) for i in range(j + 1)] for j in range(8)]
        rows = [full(left[b][j : j + 1, :]) for j in range(8)]
        inverse = [full(right[b][j : j + 1, :]) for j in range(8)]
        below = [
            [full(left[g][:, at + i : at + i + 1]) for i in range(8)]
            for g in range(b + 1, groups)
        ]
        scale = []
        for i in range(8):
            scale.append(1.0 / pivot[i][i])
            for j in range(i + 1, 8):
                factor = pivot[j][i] * scale[i]
                for k in range(i + 1, j + 1):
                    pivot[j][k] = pivot[j][k] - factor * pivot[k][i]
                rows[j] = rows[j] - factor * rows[i]
                inverse[j] = inverse[j] - factor * inverse[i]
        for g in range(b + 1, groups):
            column = below[g - b - 1]
            for i in range(8):
                factor = column[i] * scale[i]
                for k in range(i + 1, 8):
                    column[k] = column[k] - factor * pivot[k][i]
                left[g] = left[g] - factor * rows[i]
                right[g] = right[g] - factor * inverse[i]
        done, diagonal = inverse[0], pivot[0][0]
        for j in range(1, 8):
            done = jnp.where(sub == j, inverse[j], done)
            diagonal = jnp.where(sub == j, pivot[j][j], diagonal)
        inverse_ref[at : at + 8, :] = done * lax.rsqrt(diagonal)


def split(x):
    high = x.astype(jnp.bfloat16)
    return high, (x - high.astype(jnp.float32)).astype(jnp.bfloat16)


def dot_split(a, b, dims):
    (ah, al), (bh, bl) = a, b

    def dot(x, y):
        return lax.dot_general(x, y, (dims, ((), ())), preferred_element_type=jnp.float32)

    return dot(ah, bh) + (dot(ah, bl) + dot(al, bh))


def tdot(a, b):
    return lax.dot_general(
        a, b, (((0,), (0,)), ((), ())), precision=HIGHEST, preferred_element_type=jnp.float32
    )


def up8(rows):
    return -(-rows // 8) * 8


def sample_kernel(sample_ref, basis_ref, out_ref):
    rows, depth = sample_ref.shape
    cores, blocks, slab, w = basis_ref.shape
    tile = 2 * cores * slab * max(1, 128 // (cores * slab))
    per = tile // (cores * slab)
    half = depth // cores
    sums_at = half
    lifted_at = half + half // w
    projected = jnp.zeros((rows, w), jnp.float32)
    for t in range(depth // tile):
        part = jnp.concatenate(
            [basis_ref[c, t * per + i] for i in range(per) for c in range(cores)], axis=0
        )
        columns = split(sample_ref[:, t * tile : (t + 1) * tile])
        projected += dot_split(columns, split(part), ((1,), (0,)))
    lifted = jnp.sum(projected, axis=0, keepdims=True)
    pieces = split(projected)
    for t in range(depth // tile):
        columns = sample_ref[:, t * tile : (t + 1) * tile]
        core, at = t * tile // half, t * tile % half
        out_ref[core, at : at + tile, :] = dot_split(split(columns), pieces, ((0,), (0,)))
        sums = jnp.sum(columns, axis=0, keepdims=True)
        for q in range(tile // w):
            row = sums_at + at // w + q
            out_ref[core, row : row + 1, :] = sums[:, q * w : (q + 1) * w]
    for c in range(cores):
        out_ref[c, lifted_at:, :] = jnp.broadcast_to(lifted, (out_ref.shape[1] - lifted_at, w))


def halve_kernel(got_ref, out_ref):
    count, height, w = out_ref.shape
    rows = got_ref.shape[1]
    main = max(m for m in range(0, rows, w) if m + m // w < rows)
    got = sum(got_ref[i] for i in range(1, got_ref.shape[0])) + got_ref[0]
    lifted = got[main + main // w : main + main // w + 1]
    each, sums = main // count, main // w // count
    for i in range(count):
        out_ref[i, :each, :] = got[i * each : (i + 1) * each]
        out_ref[i, each : each + sums, :] = got[main + i * sums : main + (i + 1) * sums]
        out_ref[i, each + sums :, :] = jnp.broadcast_to(lifted, (height - each - sums, w))


def slab_kernel(slab, got_ref, out_ref):
    count, _, w = out_ref.shape
    got = sum(got_ref[i] for i in range(1, got_ref.shape[0])) + got_ref[0]
    main = slab * count
    sums = main // w
    lifted = got[main + sums : main + sums + 1]
    for i in range(count):
        out_ref[i, :slab, :] = got[i * slab : (i + 1) * slab]
        out_ref[i, slab : slab + sums, :] = got[main : main + sums]
        out_ref[i, slab + sums :, :] = jnp.broadcast_to(lifted, (8 - sums, w))


def image_kernel(total_rows, sums, place_ref, got_ref, spread_ref, own_ref, mean_ref):
    copies, slab, w = spread_ref.shape
    got = sum(got_ref[i] for i in range(1, got_ref.shape[0])) + got_ref[0]
    mean = got[slab : slab + 8] / total_rows
    lifted = got[slab + sums : slab + sums + 1] / total_rows
    in_row = w // slab
    at = lax.broadcasted_iota(jnp.int32, (8, w), 0)
    mine = jnp.sum(jnp.where(at == place_ref[0] // in_row, mean, 0.0), axis=0, keepdims=True)
    lane = lax.broadcasted_iota(jnp.int32, (slab, w), 1) - place_ref[0] % in_row * slab
    here = lane == lax.broadcasted_iota(jnp.int32, (slab, w), 0)
    column = jnp.sum(jnp.where(here, mine, 0.0), axis=1, keepdims=True)
    image = got[:slab] / total_rows - column * lifted
    for i in range(copies):
        spread_ref[i] = image
    own_ref[...] = image
    mean_ref[...] = mean


def gram_kernel(pieces, panel_ref, images_ref, own_ref, out_ref, gram_ref):
    panel = panel_ref[0]
    count, height, w = out_ref.shape
    half, slab = w // 2, images_ref.shape[1]
    own, after = images_ref[panel], images_ref[(panel + 1) % 4]
    last = panel == 3
    low = panel % 2
    square = tdot(own, own)
    row = lax.broadcasted_iota(jnp.int32, (half, w), 0)
    lane = lax.broadcasted_iota(jnp.int32, (half, w), 1)
    folded = jnp.where((lane > row) | (lane >= half), square[:half], pltpu.roll(square[half:], half, 1))
    below = tdot(jnp.where(last, own, after), jnp.where(last, after, own))
    across = tdot(images_ref[low + 2], images_ref[low])
    across = jnp.where(panel < 2, across[:half], across[half:])
    gram_ref[...] = jnp.concatenate([folded, below, across], axis=0)
    each = gram_ref.shape[0] // count // pieces
    for i in range(count):
        out_ref[i, :slab, :] = own_ref[...]
        for q in range(pieces):
            at, row = slab + q * each, (q * count + i) * each
            out_ref[i, at : at + each, :] = gram_ref[row : row + each, :]


def unit(w):
    row = lax.broadcasted_iota(jnp.int32, (w, w), 0)
    return row == lax.broadcasted_iota(jnp.int32, (w, w), 1)


def total(ref, at, rows):
    return sum(ref[i, at : at + rows, :] for i in range(1, ref.shape[0])) + ref[0, at : at + rows, :]


def gather_z_kernel(got_ref, mean_ref, out_ref):
    count, height, w = got_ref.shape
    share = 2 * w // count
    slab = height - share
    main = count * slab
    gram = total(got_ref, slab, share)
    for c in range(out_ref.shape[0]):
        for i in range(count):
            out_ref[c, i * slab : (i + 1) * slab, :] = got_ref[i, :slab, :]
        out_ref[c, main : main + 8, :] = mean_ref[...]
        out_ref[c, main + 8 :, :] = gram


def gather_y_kernel(main, sums, share, got_ref, out_ref):
    count, height, w = got_ref.shape
    tall = out_ref.shape[1]
    gram = total(got_ref, height - share, share)
    for c in range(out_ref.shape[0]):
        for i in range(count):
            out_ref[c, i * main : (i + 1) * main, :] = got_ref[i, :main, :]
            at = count * main + i * sums
            out_ref[c, at : at + sums, :] = got_ref[i, main : main + sums, :]
        out_ref[c, tall - share :, :] = gram


def corpus_kernel(
    main, share, lead, height_out, gram_rows, part_ref, target_ref, got_ref, corpus_ref, out_ref, diagonal_ref
):
    cores, height, w = got_ref.shape
    rows = corpus_ref.shape[0]
    tile = min(main, 4 * w)
    reduced = jnp.zeros((rows, w), jnp.float32)
    diagonal = jnp.zeros((1, w), jnp.float32)
    for c in range(cores):
        for t in range(main // tile):
            row = main + t * tile // w
            mean = jnp.concatenate(
                [got_ref[c, row + q : row + q + 1, :] for q in range(tile // w)], axis=1
            )
            at = c * main + t * tile
            centered = split(corpus_ref[:, at : at + tile] - mean)
            image = got_ref[c, t * tile : (t + 1) * tile, :]
            diagonal += jnp.sum(image * image, axis=0, keepdims=True)
            reduced += dot_split(centered, split(image), ((1,), (0,)))
    diagonal_ref[...] = jnp.broadcast_to(diagonal, diagonal_ref.shape)
    gram = total(got_ref, height - share, share)
    tall = up8(gram_rows)
    take = lax.broadcasted_iota(jnp.int32, (tall, share), 1) - part_ref[0] * gram_rows
    take = (take == lax.broadcasted_iota(jnp.int32, (tall, share), 0)).astype(jnp.float32)
    piece = jnp.dot(take, gram, precision=HIGHEST, preferred_element_type=jnp.float32)
    source = jnp.concatenate([reduced, piece], axis=0)
    shape = (out_ref.shape[0], rows + tall)
    row = lax.broadcasted_iota(jnp.int32, shape, 0)
    column = lax.broadcasted_iota(jnp.int32, shape, 1)
    place = lax.rem(row, height_out) - lead + rows
    slots = (row == target_ref[...]).astype(jnp.float32)
    shares = jnp.where(column < rows, 0.0, (place == column).astype(jnp.float32))
    out_ref[...] = jnp.dot(
        slots + shares, source, precision=HIGHEST, preferred_element_type=jnp.float32
    )


def arrange_kernel(capacity, gram_rows, got_ref, diagonal_ref, out_ref):
    count = got_ref.shape[0]
    peers = out_ref.shape[0]
    panels = 4
    lead = peers // panels * capacity
    top = count * capacity
    full = top + count * gram_rows
    for i in range(count):
        for q in range(peers // panels):
            rows = got_ref[i, q * capacity : (q + 1) * capacity, :]
            out_ref[q * panels, i * capacity : (i + 1) * capacity, :] = rows
        rows = got_ref[i, lead : lead + gram_rows, :]
        out_ref[0, top + i * gram_rows : top + (i + 1) * gram_rows, :] = rows
    for q in range(peers):
        first = q // panels * panels
        if q != first:
            out_ref[q, :top, :] = out_ref[first, :top, :]
        if q:
            out_ref[q, top:full, :] = out_ref[0, top:full, :]
        out_ref[q, full:, :] = diagonal_ref[...]


def solve_kernel(
    counts, panel_ref, got_ref, out_ref, work_ref, inverse_ref, stacked_ref, own_ref
):
    blocks, _, w = work_ref.shape
    kept = out_ref.shape[0]
    size = blocks * w
    half = w // 2
    ny, nz, nc = counts
    top = kept // (ny * nc)
    share = 2 * w // (ny * nc)
    row = lax.broadcasted_iota(jnp.int32, (half, w), 0)
    lane = lax.broadcasted_iota(jnp.int32, (half, w), 1)
    for k in range(blocks):
        for q in range(ny * nc):
            source = q * blocks + k
            stacked_ref[k, q * share : (q + 1) * share, :] = got_ref[source, top : top + share, :]
            at = size + q * top
            work_ref[k, at : at + top, :] = got_ref[source, :top, :]
        folded = stacked_ref[k, :half, :]
        upper = jnp.where((lane > row) | (lane >= half), folded, 0.0)
        moved = pltpu.roll(folded, half, 1)
        lower = jnp.where((lane >= half) & (lane - half < row), moved, 0.0)
        square = jnp.concatenate([upper, lower], axis=0)
        diagonal = got_ref[k, top + share : top + share + 1, :]
        square = square + square.T + jnp.where(unit(w), diagonal, 0.0)
        work_ref[k, k * w : (k + 1) * w, :] = square
        if k < 3:
            work_ref[k, (k + 1) * w : (k + 2) * w, :] = stacked_ref[k, half : half + w, :]
    work_ref[0, 3 * w : 4 * w, :] = stacked_ref[3, half : half + w, :]
    for k in range(2):
        for part in range(2):
            at = (k + 2) * w + part * half
            work_ref[k, at : at + half, :] = stacked_ref[k + 2 * part, half + w : 2 * w, :]

    def finish(k):
        solved = dot_t(work_ref[k, (k + 1) * w :, :], inverse_ref[...])
        for m in range(k + 1, blocks):
            at = (m - k - 1) * w
            work_ref[m, m * w :, :] -= dot_t(solved[at:], solved[at : at + w])

        @pl.when(panel_ref[0] == k)
        def _():
            own_ref[...] = solved[-kept:]

    def step(k, carry):
        invert_factor(work_ref.at[k, pl.ds(pl.multiple_of(k * w, w), w)], inverse_ref)
        for q in range(blocks):
            pl.when(k == q)(functools.partial(finish, q))
        return carry

    lax.fori_loop(0, blocks, step, 0)
    slots = kept // (ny * nz * nc)
    for i in range(ny * nz * nc):
        y, z, core = i // (nz * nc), i // nc % nz, i % nc
        at = ((y * nc + core) * nz + z) * slots
        out_ref[i * slots : (i + 1) * slots, :] = own_ref[at : at + slots, :]


def call(kernel, shapes, *operands, scalars=0, scratch=(), flops=0):
    vmem = pl.BlockSpec(memory_space=pltpu.VMEM)
    smem = pl.BlockSpec(memory_space=pltpu.SMEM)
    outs = [jax.ShapeDtypeStruct(shape, jnp.float32) for shape in shapes]
    moved = 4 * sum(x.size for x in (*operands, *outs))
    got = pl.pallas_call(
        kernel,
        out_shape=outs,
        in_specs=[smem] * scalars + [vmem] * (len(operands) - scalars),
        out_specs=[vmem] * len(outs),
        scratch_shapes=[pltpu.VMEM(shape, jnp.float32) for shape in scratch],
        compiler_params=pltpu.CompilerParams(vmem_limit_bytes=40 << 20),
        cost_estimate=pl.CostEstimate(flops=flops, bytes_accessed=moved, transcendentals=0),
    )(*operands)
    return got if len(outs) > 1 else got[0]


def body(sample, start_basis, corpus, owner_shard):
    ny, nz, nc, panels = (lax.axis_size(name) for name in (*DP, "panel"))
    owners = ny * nz * nc
    slab, w = start_basis.shape
    depth = slab * owners
    rows = sample.shape[0]
    total_rows = rows * owners
    panel = lax.axis_index("panel").astype(jnp.int32).reshape(1)

    basis = spread(spread(spread(start_basis, "z"), "y"), "core")
    basis = basis.reshape(nc, ny * nz, slab, w)

    height = up8(depth // nc + depth // nc // w + 1)
    message = call(sample_kernel, [(nc, height, w)], sample, basis, flops=4 * rows * depth * w)
    main = depth // nc // ny
    message = call(halve_kernel, [(ny, up8(main + main // w + 1), w)], swap(message, "core"))
    message = call(
        functools.partial(slab_kernel, slab), [(nz, slab + 8, w)], swap(message, "y")
    )
    sums = main // w
    images, own, mean = call(
        functools.partial(image_kernel, float(total_rows), sums),
        [(panels, slab, w), (slab, w), (8, w)],
        lax.axis_index("z").astype(jnp.int32).reshape(1),
        swap(message, "z"),
        scalars=1,
    )

    share = 2 * w // nz
    message = call(
        functools.partial(gram_kernel, ny * nc),
        [(nz, slab + share, w)],
        panel,
        swap(images, "panel"),
        own,
        scalars=1,
        scratch=[(2 * w, w)],
    )
    message = call(gather_z_kernel, [(ny, main + 8 + share, w)], swap(message, "z"), mean)
    message = call(
        functools.partial(gather_y_kernel, main, sums, share),
        [(nc, ny * main + up8(ny * sums) + share, w)],
        swap(message, "y"),
    )

    corpus_rows = corpus.shape[0]
    capacity = max(2, 2 * corpus_rows // owners)
    gram_rows = 2 * w // owners
    lead = ny * nc * capacity
    height = up8(lead + gram_rows)
    owner_ids = owner_shard[:, 0]
    choose = (owner_ids[:, None] == jnp.arange(owners, dtype=jnp.int32)[None, :]).astype(jnp.int32)
    running = jnp.cumsum(choose, axis=0)
    slot_index = jnp.sum(running * choose, axis=1) - 1
    plane = owner_ids // (nz * nc) * nc + owner_ids % nc
    target = owner_ids // nc % nz * height + plane * capacity + slot_index
    target = jnp.pad(target, (0, up8(gram_rows)), constant_values=-1)[None, :]
    part = lax.axis_index("y") * nc + lax.axis_index("core")
    part = part.astype(jnp.int32).reshape(1)
    outgoing, diagonal = call(
        functools.partial(corpus_kernel, ny * main, share, lead, height, gram_rows),
        [(nz * height, w), (8, w)],
        part,
        target,
        swap(message, "core"),
        corpus,
        scalars=1,
        flops=2 * corpus_rows * depth * w,
    )
    message = call(
        functools.partial(arrange_kernel, capacity, gram_rows),
        [(ny * nc * panels, nz * (capacity + gram_rows) + 8, w)],
        swap(outgoing.reshape(nz, height, w), "z"),
        diagonal,
    )
    slots = owners * capacity
    return call(
        functools.partial(solve_kernel, (ny, nz, nc)),
        [(slots, w)],
        panel,
        swap(message, ("y", "core", "panel")),
        scalars=1,
        scratch=[(panels, panels * w + slots, w), (w, w), (panels, 2 * w, w), (slots, w)],
        flops=panels * panels * w * w * (panels * w + slots),
    )


def solution(mesh):
    y, z, core, panel = 4, 16, 2, mesh.shape["panel"]
    fine = Mesh(mesh.devices.reshape(y, z, core, panel), (*DP, "panel"))
    placed = (P(DP, None), P(DP, "panel"), P(DP, None), P(DP, None))
    return jax.shard_map(
        body, mesh=fine, in_specs=placed, out_specs=P(DP, "panel"), check_vma=False
    )
```

```python
import functools

import jax
import jax.numpy as jnp
from jax import lax
from jax.experimental import pallas as pl
from jax.experimental.pallas import tpu as pltpu
from jax.sharding import Mesh
from jax.sharding import PartitionSpec as P

DP = ("y", "z", "core")
HIGHEST = lax.Precision.HIGHEST


def swap(parts, axis):
    return lax.all_to_all(parts, axis, 0, 0, tiled=True)


def spread(block, axis):
    return swap(jnp.broadcast_to(block[None], (lax.axis_size(axis), *block.shape)), axis)


def dot_t(a, b):
    return lax.dot_general(
        a, b, (((1,), (1,)), ((), ())), precision=HIGHEST, preferred_element_type=jnp.float32
    )


def invert_factor(block_ref, inverse_ref):
    n = block_ref.shape[0]
    groups = n // 8
    sub = lax.broadcasted_iota(jnp.int32, (8, n), 0)
    lane = lax.broadcasted_iota(jnp.int32, (8, n), 1)

    def full(x):
        return jnp.broadcast_to(x, (8, n))

    left = [block_ref[8 * g : 8 * g + 8, :] for g in range(groups)]
    right = [(lane == sub + 8 * g).astype(jnp.float32) for g in range(groups)]
    for b in range(groups):
        at = 8 * b
        columns = [full(left[b][:, at + i : at + i + 1]) for i in range(8)]
        pivot = [[full(columns[i][j : j + 1, :]) for i in range(j + 1)] for j in range(8)]
        rows = [full(left[b][j : j + 1, :]) for j in range(8)]
        inverse = [full(right[b][j : j + 1, :]) for j in range(8)]
        below = [
            [full(left[g][:, at + i : at + i + 1]) for i in range(8)]
            for g in range(b + 1, groups)
        ]
        scale = []
        for i in range(8):
            if i % 2 == 0:
                p, q, r = pivot[i][i], pivot[i + 1][i], pivot[i + 1][i + 1]
                scale += [1.0 / p, p * (1.0 / (p * r - q * q))]
            for j in range(i + 1, 8):
                factor = pivot[j][i] * scale[i]
                for k in range(i + 1, j + 1):
                    pivot[j][k] = pivot[j][k] - factor * pivot[k][i]
                rows[j] = rows[j] - factor * rows[i]
                inverse[j] = inverse[j] - factor * inverse[i]
        for g in range(b + 1, groups):
            column = below[g - b - 1]
            for i in range(8):
                factor = column[i] * scale[i]
                for k in range(i + 1, 8):
                    column[k] = column[k] - factor * pivot[k][i]
                left[g] = left[g] - factor * rows[i]
                right[g] = right[g] - factor * inverse[i]
        done, diagonal = inverse[0], pivot[0][0]
        for j in range(1, 8):
            done = jnp.where(sub == j, inverse[j], done)
            diagonal = jnp.where(sub == j, pivot[j][j], diagonal)
        inverse_ref[at : at + 8, :] = done * lax.rsqrt(diagonal)


def split(x):
    high = x.astype(jnp.bfloat16)
    return high, (x - high.astype(jnp.float32)).astype(jnp.bfloat16)


def dot_split(a, b, dims):
    (ah, al), (bh, bl) = a, b

    def dot(x, y):
        return lax.dot_general(x, y, (dims, ((), ())), preferred_element_type=jnp.float32)

    return dot(ah, bh) + (dot(ah, bl) + dot(al, bh))


def tdot(a, b):
    return lax.dot_general(
        a, b, (((0,), (0,)), ((), ())), precision=HIGHEST, preferred_element_type=jnp.float32
    )


def up8(rows):
    return -(-rows // 8) * 8


def sample_kernel(sample_ref, basis_ref, out_ref):
    rows, depth = sample_ref.shape
    cores, blocks, slab, w = basis_ref.shape
    tile = 2 * cores * slab * max(1, 128 // (cores * slab))
    per = tile // (cores * slab)
    half = depth // cores
    sums_at = half
    lifted_at = half + half // w
    projected = jnp.zeros((rows, w), jnp.float32)
    for t in range(depth // tile):
        part = jnp.concatenate(
            [basis_ref[c, t * per + i] for i in range(per) for c in range(cores)], axis=0
        )
        columns = split(sample_ref[:, t * tile : (t + 1) * tile])
        projected += dot_split(columns, split(part), ((1,), (0,)))
    lifted = jnp.sum(projected, axis=0, keepdims=True)
    pieces = split(projected)
    for t in range(depth // tile):
        columns = sample_ref[:, t * tile : (t + 1) * tile]
        core, at = t * tile // half, t * tile % half
        out_ref[core, at : at + tile, :] = dot_split(split(columns), pieces, ((0,), (0,)))
        sums = jnp.sum(columns, axis=0, keepdims=True)
        for q in range(tile // w):
            row = sums_at + at // w + q
            out_ref[core, row : row + 1, :] = sums[:, q * w : (q + 1) * w]
    for c in range(cores):
        out_ref[c, lifted_at:, :] = jnp.broadcast_to(lifted, (out_ref.shape[1] - lifted_at, w))


def halve_kernel(got_ref, out_ref):
    count, height, w = out_ref.shape
    rows = got_ref.shape[1]
    main = max(m for m in range(0, rows, w) if m + m // w < rows)
    got = sum(got_ref[i] for i in range(1, got_ref.shape[0])) + got_ref[0]
    lifted = got[main + main // w : main + main // w + 1]
    each, sums = main // count, main // w // count
    for i in range(count):
        out_ref[i, :each, :] = got[i * each : (i + 1) * each]
        out_ref[i, each : each + sums, :] = got[main + i * sums : main + (i + 1) * sums]
        out_ref[i, each + sums :, :] = jnp.broadcast_to(lifted, (height - each - sums, w))


def slab_kernel(slab, got_ref, out_ref):
    count, _, w = out_ref.shape
    got = sum(got_ref[i] for i in range(1, got_ref.shape[0])) + got_ref[0]
    main = slab * count
    sums = main // w
    lifted = got[main + sums : main + sums + 1]
    for i in range(count):
        out_ref[i, :slab, :] = got[i * slab : (i + 1) * slab]
        out_ref[i, slab : slab + sums, :] = got[main : main + sums]
        out_ref[i, slab + sums :, :] = jnp.broadcast_to(lifted, (8 - sums, w))


def image_kernel(total_rows, sums, place_ref, got_ref, spread_ref, own_ref, mean_ref):
    copies, slab, w = spread_ref.shape
    got = sum(got_ref[i] for i in range(1, got_ref.shape[0])) + got_ref[0]
    mean = got[slab : slab + 8] / total_rows
    lifted = got[slab + sums : slab + sums + 1] / total_rows
    in_row = w // slab
    at = lax.broadcasted_iota(jnp.int32, (8, w), 0)
    mine = jnp.sum(jnp.where(at == place_ref[0] // in_row, mean, 0.0), axis=0, keepdims=True)
    lane = lax.broadcasted_iota(jnp.int32, (slab, w), 1) - place_ref[0] % in_row * slab
    here = lane == lax.broadcasted_iota(jnp.int32, (slab, w), 0)
    column = jnp.sum(jnp.where(here, mine, 0.0), axis=1, keepdims=True)
    image = got[:slab] / total_rows - column * lifted
    for i in range(copies):
        spread_ref[i] = image
    own_ref[...] = image
    mean_ref[...] = mean


def gram_kernel(pieces, panel_ref, images_ref, own_ref, out_ref, gram_ref):
    panel = panel_ref[0]
    count, height, w = out_ref.shape
    half, slab = w // 2, images_ref.shape[1]
    own, after = images_ref[panel], images_ref[(panel + 1) % 4]
    last = panel == 3
    low = panel % 2
    square = tdot(own, own)
    row = lax.broadcasted_iota(jnp.int32, (half, w), 0)
    lane = lax.broadcasted_iota(jnp.int32, (half, w), 1)
    folded = jnp.where((lane > row) | (lane >= half), square[:half], pltpu.roll(square[half:], half, 1))
    below = tdot(jnp.where(last, own, after), jnp.where(last, after, own))
    across = tdot(images_ref[low + 2], images_ref[low])
    across = jnp.where(panel < 2, across[:half], across[half:])
    gram_ref[...] = jnp.concatenate([folded, below, across], axis=0)
    each = gram_ref.shape[0] // count // pieces
    for i in range(count):
        out_ref[i, :slab, :] = own_ref[...]
        for q in range(pieces):
            at, row = slab + q * each, (q * count + i) * each
            out_ref[i, at : at + each, :] = gram_ref[row : row + each, :]


def unit(w):
    row = lax.broadcasted_iota(jnp.int32, (w, w), 0)
    return row == lax.broadcasted_iota(jnp.int32, (w, w), 1)


def total(ref, at, rows):
    return sum(ref[i, at : at + rows, :] for i in range(1, ref.shape[0])) + ref[0, at : at + rows, :]


def gather_z_kernel(got_ref, mean_ref, out_ref):
    count, height, w = got_ref.shape
    share = 2 * w // count
    slab = height - share
    main = count * slab
    gram = total(got_ref, slab, share)
    for c in range(out_ref.shape[0]):
        for i in range(count):
            out_ref[c, i * slab : (i + 1) * slab, :] = got_ref[i, :slab, :]
        out_ref[c, main : main + 8, :] = mean_ref[...]
        out_ref[c, main + 8 :, :] = gram


def gather_y_kernel(main, sums, share, got_ref, out_ref):
    count, height, w = got_ref.shape
    tall = out_ref.shape[1]
    gram = total(got_ref, height - share, share)
    for c in range(out_ref.shape[0]):
        for i in range(count):
            out_ref[c, i * main : (i + 1) * main, :] = got_ref[i, :main, :]
            at = count * main + i * sums
            out_ref[c, at : at + sums, :] = got_ref[i, main : main + sums, :]
        out_ref[c, tall - share :, :] = gram


def corpus_kernel(
    main, share, lead, height_out, gram_rows, part_ref, target_ref, got_ref, corpus_ref, out_ref, diagonal_ref
):
    cores, height, w = got_ref.shape
    rows = corpus_ref.shape[0]
    tile = min(main, 4 * w)
    reduced = jnp.zeros((rows, w), jnp.float32)
    diagonal = jnp.zeros((1, w), jnp.float32)
    for c in range(cores):
        for t in range(main // tile):
            row = main + t * tile // w
            mean = jnp.concatenate(
                [got_ref[c, row + q : row + q + 1, :] for q in range(tile // w)], axis=1
            )
            at = c * main + t * tile
            centered = split(corpus_ref[:, at : at + tile] - mean)
            image = got_ref[c, t * tile : (t + 1) * tile, :]
            diagonal += jnp.sum(image * image, axis=0, keepdims=True)
            reduced += dot_split(centered, split(image), ((1,), (0,)))
    diagonal_ref[...] = jnp.broadcast_to(diagonal, diagonal_ref.shape)
    gram = total(got_ref, height - share, share)
    tall = up8(gram_rows)
    take = lax.broadcasted_iota(jnp.int32, (tall, share), 1) - part_ref[0] * gram_rows
    take = (take == lax.broadcasted_iota(jnp.int32, (tall, share), 0)).astype(jnp.float32)
    piece = jnp.dot(take, gram, precision=HIGHEST, preferred_element_type=jnp.float32)
    source = jnp.concatenate([reduced, piece], axis=0)
    shape = (out_ref.shape[0], rows + tall)
    row = lax.broadcasted_iota(jnp.int32, shape, 0)
    column = lax.broadcasted_iota(jnp.int32, shape, 1)
    place = lax.rem(row, height_out) - lead + rows
    slots = (row == target_ref[...]).astype(jnp.float32)
    shares = jnp.where(column < rows, 0.0, (place == column).astype(jnp.float32))
    out_ref[...] = jnp.dot(
        slots + shares, source, precision=HIGHEST, preferred_element_type=jnp.float32
    )


def arrange_kernel(capacity, gram_rows, got_ref, diagonal_ref, out_ref):
    count = got_ref.shape[0]
    peers = out_ref.shape[0]
    panels = 4
    lead = peers // panels * capacity
    top = count * capacity
    full = top + count * gram_rows
    for i in range(count):
        for q in range(peers // panels):
            rows = got_ref[i, q * capacity : (q + 1) * capacity, :]
            out_ref[q * panels, i * capacity : (i + 1) * capacity, :] = rows
        rows = got_ref[i, lead : lead + gram_rows, :]
        out_ref[0, top + i * gram_rows : top + (i + 1) * gram_rows, :] = rows
    for q in range(peers):
        first = q // panels * panels
        if q != first:
            out_ref[q, :top, :] = out_ref[first, :top, :]
        if q:
            out_ref[q, top:full, :] = out_ref[0, top:full, :]
        out_ref[q, full:, :] = diagonal_ref[...]


def solve_kernel(
    counts, panel_ref, got_ref, out_ref, work_ref, inverse_ref, stacked_ref, own_ref
):
    blocks, _, w = work_ref.shape
    kept = out_ref.shape[0]
    size = blocks * w
    half = w // 2
    ny, nz, nc = counts
    top = kept // (ny * nc)
    share = 2 * w // (ny * nc)
    row = lax.broadcasted_iota(jnp.int32, (half, w), 0)
    lane = lax.broadcasted_iota(jnp.int32, (half, w), 1)
    for k in range(blocks):
        for q in range(ny * nc):
            source = q * blocks + k
            stacked_ref[k, q * share : (q + 1) * share, :] = got_ref[source, top : top + share, :]
            at = size + q * top
            work_ref[k, at : at + top, :] = got_ref[source, :top, :]
        folded = stacked_ref[k, :half, :]
        upper = jnp.where((lane > row) | (lane >= half), folded, 0.0)
        moved = pltpu.roll(folded, half, 1)
        lower = jnp.where((lane >= half) & (lane - half < row), moved, 0.0)
        square = jnp.concatenate([upper, lower], axis=0)
        diagonal = got_ref[k, top + share : top + share + 1, :]
        square = square + square.T + jnp.where(unit(w), diagonal, 0.0)
        work_ref[k, k * w : (k + 1) * w, :] = square
        if k < 3:
            work_ref[k, (k + 1) * w : (k + 2) * w, :] = stacked_ref[k, half : half + w, :]
    work_ref[0, 3 * w : 4 * w, :] = stacked_ref[3, half : half + w, :]
    for k in range(2):
        for part in range(2):
            at = (k + 2) * w + part * half
            work_ref[k, at : at + half, :] = stacked_ref[k + 2 * part, half + w : 2 * w, :]
    roots = [lax.rsqrt(got_ref[k, top + share : top + share + 1, :]) for k in range(blocks)]
    turned = [jnp.sum(jnp.where(unit(w), x, 0.0), axis=1, keepdims=True) for x in roots]
    for k in range(blocks):
        for m in range(k, blocks):
            block = work_ref[k, m * w : (m + 1) * w, :]
            work_ref[k, m * w : (m + 1) * w, :] = block * roots[k] * turned[m]
        work_ref[k, size:, :] = work_ref[k, size:, :] * roots[k]

    def finish(k):
        solved = dot_t(work_ref[k, (k + 1) * w :, :], inverse_ref[...])
        for m in range(k + 1, blocks):
            at = (m - k - 1) * w
            work_ref[m, m * w :, :] -= dot_t(solved[at:], solved[at : at + w])

        @pl.when(panel_ref[0] == k)
        def _():
            own_ref[...] = solved[-kept:]

    def step(k, carry):
        invert_factor(work_ref.at[k, pl.ds(pl.multiple_of(k * w, w), w)], inverse_ref)
        for q in range(blocks):
            pl.when(k == q)(functools.partial(finish, q))
        return carry

    lax.fori_loop(0, blocks, step, 0)
    slots = kept // (ny * nz * nc)
    for i in range(ny * nz * nc):
        y, z, core = i // (nz * nc), i // nc % nz, i % nc
        at = ((y * nc + core) * nz + z) * slots
        out_ref[i * slots : (i + 1) * slots, :] = own_ref[at : at + slots, :]


def call(kernel, shapes, *operands, scalars=0, scratch=(), flops=0):
    vmem = pl.BlockSpec(memory_space=pltpu.VMEM)
    smem = pl.BlockSpec(memory_space=pltpu.SMEM)
    outs = [jax.ShapeDtypeStruct(shape, jnp.float32) for shape in shapes]
    moved = 4 * sum(x.size for x in (*operands, *outs))
    got = pl.pallas_call(
        kernel,
        out_shape=outs,
        in_specs=[smem] * scalars + [vmem] * (len(operands) - scalars),
        out_specs=[vmem] * len(outs),
        scratch_shapes=[pltpu.VMEM(shape, jnp.float32) for shape in scratch],
        compiler_params=pltpu.CompilerParams(vmem_limit_bytes=40 << 20),
        cost_estimate=pl.CostEstimate(flops=flops, bytes_accessed=moved, transcendentals=0),
    )(*operands)
    return got if len(outs) > 1 else got[0]


def body(sample, start_basis, corpus, owner_shard):
    ny, nz, nc, panels = (lax.axis_size(name) for name in (*DP, "panel"))
    owners = ny * nz * nc
    slab, w = start_basis.shape
    depth = slab * owners
    rows = sample.shape[0]
    total_rows = rows * owners
    panel = lax.axis_index("panel").astype(jnp.int32).reshape(1)

    basis = spread(spread(spread(start_basis, "z"), "y"), "core")
    basis = basis.reshape(nc, ny * nz, slab, w)

    height = up8(depth // nc + depth // nc // w + 1)
    message = call(sample_kernel, [(nc, height, w)], sample, basis, flops=4 * rows * depth * w)
    main = depth // nc // ny
    message = call(halve_kernel, [(ny, up8(main + main // w + 1), w)], swap(message, "core"))
    message = call(
        functools.partial(slab_kernel, slab), [(nz, slab + 8, w)], swap(message, "y")
    )
    sums = main // w
    images, own, mean = call(
        functools.partial(image_kernel, float(total_rows), sums),
        [(panels, slab, w), (slab, w), (8, w)],
        lax.axis_index("z").astype(jnp.int32).reshape(1),
        swap(message, "z"),
        scalars=1,
    )

    share = 2 * w // nz
    message = call(
        functools.partial(gram_kernel, ny * nc),
        [(nz, slab + share, w)],
        panel,
        swap(images, "panel"),
        own,
        scalars=1,
        scratch=[(2 * w, w)],
    )
    message = call(gather_z_kernel, [(ny, main + 8 + share, w)], swap(message, "z"), mean)
    message = call(
        functools.partial(gather_y_kernel, main, sums, share),
        [(nc, ny * main + up8(ny * sums) + share, w)],
        swap(message, "y"),
    )

    corpus_rows = corpus.shape[0]
    capacity = max(2, 2 * corpus_rows // owners)
    gram_rows = 2 * w // owners
    lead = ny * nc * capacity
    height = up8(lead + gram_rows)
    owner_ids = owner_shard[:, 0]
    choose = (owner_ids[:, None] == jnp.arange(owners, dtype=jnp.int32)[None, :]).astype(jnp.int32)
    running = jnp.cumsum(choose, axis=0)
    slot_index = jnp.sum(running * choose, axis=1) - 1
    plane = owner_ids // (nz * nc) * nc + owner_ids % nc
    target = owner_ids // nc % nz * height + plane * capacity + slot_index
    target = jnp.pad(target, (0, up8(gram_rows)), constant_values=-1)[None, :]
    part = lax.axis_index("y") * nc + lax.axis_index("core")
    part = part.astype(jnp.int32).reshape(1)
    outgoing, diagonal = call(
        functools.partial(corpus_kernel, ny * main, share, lead, height, gram_rows),
        [(nz * height, w), (8, w)],
        part,
        target,
        swap(message, "core"),
        corpus,
        scalars=1,
        flops=2 * corpus_rows * depth * w,
    )
    message = call(
        functools.partial(arrange_kernel, capacity, gram_rows),
        [(ny * nc * panels, nz * (capacity + gram_rows) + 8, w)],
        swap(outgoing.reshape(nz, height, w), "z"),
        diagonal,
    )
    slots = owners * capacity
    return call(
        functools.partial(solve_kernel, (ny, nz, nc)),
        [(slots, w)],
        panel,
        swap(message, ("y", "core", "panel")),
        scalars=1,
        scratch=[(panels, panels * w + slots, w), (w, w), (panels, 2 * w, w), (slots, w)],
        flops=panels * panels * w * w * (panels * w + slots),
    )


def solution(mesh):
    y, z, core, panel = 4, 16, 2, mesh.shape["panel"]
    fine = Mesh(mesh.devices.reshape(y, z, core, panel), (*DP, "panel"))
    placed = (P(DP, None), P(DP, "panel"), P(DP, None), P(DP, None))
    return jax.shard_map(
        body, mesh=fine, in_specs=placed, out_specs=P(DP, "panel"), check_vma=False
    )
```
